128 devices in a mesh: dp: 16 (over z_hi, x, core), tensor: 8 (over y, z_lo).
Axes of the slice: x: 4, y: 4, z: 4 (z_hi: 2, z_lo: 2; z = z_hi * 2 + z_lo), core: 2. Of those that a mesh axis runs over, the one named last changes fastest.
Arguments:
- tokens: bfloat16 [16384, 4096], P(('dp', 'tensor')), may hold values from -6 to 6
- in_weight: bfloat16 [4096, 20608], P(('dp', 'tensor')), may hold values from -0.09375 to 0.09375
- group_order: int32 [8], replicated, may hold values from 0 to 7, each once
- head_order: int32 [8, 16], replicated, may hold values from 0 to 15, each once within a row
- conv_x: float32 [4, 8192], P(None, 'tensor'), may hold values from -3 to 3
- conv_bc: float32 [4, 4096], P(None, 'tensor'), may hold values from -3 to 3
- dt_bias: float32 [128], P('tensor'), may hold values from -3 to 1
Outputs:
- gated: bfloat16 [16384, 8192], P('dp', 'tensor')
- bc_out: bfloat16 [16384, 4096], P('dp', 'tensor')
- dt_out: float32 [16384, 128], P('dp', 'tensor')
The draws below stay inside these ranges and needn't reach their ends.
Inputs may be any that keep to these rules, and one draw needn't show every extreme that they name: `group_order`: each value once. `head_order`: each row holds each value once.
All inputs are finite; a program needn't handle non-finite values.
Results may differ from the reference program's by a relative error of at most 0.0062.
Values may be sent and summed in bfloat16 or wider, within the bound.
A program may use at most 128 MiB of HBM per device.

```python
import jax
import jax.numpy as jnp
from jax import lax

D = 4096
P_SIZE = 64
HPG = 16
N = 256
KW = 4
G = 8
HEADS = 128
GW = 2576
TOKENS = 16384


def block_scale(rng, shape, shards, low, high):
    factor_of, own = 1.0, jax.random.fold_in(rng, 6)
    for dim, shards_of in shards:
        heights = jnp.exp(jax.random.uniform(jax.random.fold_in(own, dim), (shards_of,), jnp.float32, low / len(shards), high / len(shards)))
        factor_of = factor_of * jnp.repeat(heights, shape[dim] // shards_of).reshape([-1 if axis == dim else 1 for axis in range(len(shape))])
    return factor_of


def centred(own_key, shape, spread, most, pieces=(), kind=jnp.bfloat16):
    loudness = block_scale(own_key, shape, pieces, -0.22, 0.18) if pieces else 1.0
    result = jax.random.normal(own_key, shape, jnp.float32) * spread * loudness
    return jnp.minimum(jnp.maximum(result, -most), most).astype(kind)


def setup_inputs(seed: int = 0) -> dict:
    keys = jax.random.split(jax.random.key(seed), 8)
    return {
        "tokens": centred(keys[0], (TOKENS, D), 1.0, 6.0, ((0, 128),)),
        "in_weight": centred(keys[1], (D, G * GW), D ** -0.5, 0.09375, ((0, 128),)),
        "group_order": jax.random.permutation(keys[2], G).astype(jnp.int32),
        "head_order": jax.vmap(lambda own: jax.random.permutation(own, HPG))(jax.random.split(keys[3], G)).reshape((G, HPG)).astype(jnp.int32),
        "conv_x": centred(keys[4], (KW, HEADS * P_SIZE), 0.5, 3.0, ((1, 8),), jnp.float32),
        "conv_bc": centred(keys[5], (KW, G * 2 * N), 0.5, 3.0, ((1, 8),), jnp.float32),
        "dt_bias": jnp.clip(-3.0 + 4.0 * jax.random.uniform(keys[6], (HEADS,), jnp.float32) ** block_scale(keys[6], (HEADS,), ((0, 8),), -0.2, 0.2), -3.0, 1.0),
    }


def permute_block(column_block, head_perm):
    row_count = column_block.shape[0]
    head_cols = HPG * P_SIZE
    gate_part = jnp.take(column_block[:, :head_cols].reshape(row_count, HPG, P_SIZE), head_perm, axis=1).reshape(row_count, head_cols)
    value_part = jnp.take(column_block[:, head_cols:2 * head_cols].reshape(row_count, HPG, P_SIZE), head_perm, axis=1).reshape(row_count, head_cols)
    state_part = column_block[:, 2 * head_cols:2 * head_cols + 2 * N]
    step_part = jnp.take(column_block[:, 2 * head_cols + 2 * N:], head_perm, axis=1)
    return jnp.concatenate([gate_part, value_part, state_part, step_part], axis=1)


def reference(tokens, in_weight, group_order, head_order, conv_x, conv_bc, dt_bias):
    head_cols = HPG * P_SIZE

    def one_slot(slot_index):
        group_pick = group_order[slot_index]
        column_block = lax.dynamic_slice_in_dim(in_weight, (group_pick * GW).astype(jnp.int32), GW, 1)
        column_block = permute_block(column_block, head_order[slot_index])
        projected = jnp.dot(tokens, column_block, preferred_element_type=jnp.float32).astype(jnp.bfloat16)
        gate_raw = projected[:, :head_cols]
        mixing = projected[:, head_cols:2 * head_cols + 2 * N]
        step_raw = projected[:, 2 * head_cols + 2 * N:]
        taps_x = lax.dynamic_slice_in_dim(conv_x, (slot_index * head_cols).astype(jnp.int32), head_cols, 1)
        taps_bc = lax.dynamic_slice_in_dim(conv_bc, (slot_index * 2 * N).astype(jnp.int32), 2 * N, 1)
        kernel = jnp.concatenate([taps_x, taps_bc], axis=1).astype(jnp.float32)
        extended = jnp.concatenate([jnp.zeros((KW - 1, mixing.shape[1]), jnp.bfloat16), mixing], axis=0)
        running = kernel[0] * extended[0:TOKENS].astype(jnp.float32)
        for position in range(1, KW):
            running = running + kernel[position] * extended[position:position + TOKENS].astype(jnp.float32)
        gated = (jax.nn.silu(running[:, :head_cols]) * jax.nn.silu(gate_raw.astype(jnp.float32))).astype(jnp.bfloat16)
        states = jax.nn.silu(running[:, head_cols:]).astype(jnp.bfloat16)
        bias_part = lax.dynamic_slice_in_dim(dt_bias, (slot_index * HPG).astype(jnp.int32), HPG, 0)
        steps_out = jax.nn.softplus(step_raw.astype(jnp.float32) + bias_part)
        return gated, states, steps_out

    gated, states, steps_out = lax.map(one_slot, jnp.arange(G, dtype=jnp.int32))
    gated = jnp.transpose(gated, (1, 0, 2)).reshape(TOKENS, G * head_cols)
    states = jnp.transpose(states, (1, 0, 2)).reshape(TOKENS, G * 2 * N)
    steps_out = jnp.transpose(steps_out, (1, 0, 2)).reshape(TOKENS, G * HPG)
    return gated, states, steps_out
```

```python
import functools

import jax
import jax.numpy as jnp
from jax import lax
from jax.experimental import pallas as pl
from jax.experimental.pallas import tpu as pltpu
from jax.sharding import PartitionSpec as P

MESH = pl.DeviceIdType.MESH
HEAD = 64
HPG = 16
N = 256
GW = 2 * HPG * HEAD + 2 * N + HPG
D = 4096
ROWS = 1024
TOK = 128
KB = 256
KR = 32
GRP = 256
HALO = 16
CW = 512
ORDER = ("dt", 0, 1, 2, 3, 4)


def arrange(group_order, head_order, w_own, stage, stage_dt, lined):
    lane = lax.broadcasted_iota(jnp.int32, (KR, 128), 1)

    def line_up(slot):
        group = group_order[slot]
        for part in range(4):
            start = pl.multiple_of((20 * group + 5 * part) * 128, 128)
            wide = pltpu.roll(w_own[:, pl.ds(start, 768)].astype(jnp.float32), (768 - 16 * group) % 768, 1)
            lined[:, 640 * part : 640 * part + 640] = wide[:, :640]
        start = pl.multiple_of((20 * group + 20) * 128, 128)
        tile = pltpu.roll(w_own[:, pl.ds(start, 128)].astype(jnp.float32), (128 - 16 * group) % 128, 1)
        lined[:, 2560:2688] = jnp.where(lane < HPG, tile, 0.0)

    def head_tile(slot, base, first):
        parts = []
        for half in range(2):
            picked = head_order[slot, first + half]
            start = pl.multiple_of(base + 128 * (picked >> 1), 128)
            tile = lined[:, pl.ds(start, 128)]
            parts.append(jnp.where((picked & 1) == half, tile, pltpu.roll(tile, HEAD, 1)))
        return jnp.where(lane < HEAD, parts[0], parts[1]).astype(jnp.bfloat16)

    def make(chunk, slot, store):
        if chunk == "dt":
            source = jnp.full((128, 128), 128, jnp.int32)
            across = lax.broadcasted_iota(jnp.int32, (128, 128), 1)
            for j in range(HPG):
                source = jnp.where(across == j, head_order[slot, j], source)
            down = lax.broadcasted_iota(jnp.int32, (128, 128), 0)
            pick = (down == source).astype(jnp.float32).astype(jnp.bfloat16)
            tile = lined[:, 2560:2688].astype(jnp.bfloat16)
            store(0, jnp.dot(tile, pick, preferred_element_type=jnp.float32).astype(jnp.bfloat16))
        elif chunk == 4:
            for tile in range(4):
                store(tile, lined[:, 2048 + 128 * tile : 2176 + 128 * tile].astype(jnp.bfloat16))
        else:
            for part in range(2):
                for pair in range(2):
                    store(2 * part + pair, head_tile(slot, 1024 * part, 4 * chunk + 2 * pair))

    def body(slot, carry):
        line_up(slot)

        def store_dt(tile, value):
            stage_dt[slot] = value

        make("dt", slot, store_dt)
        for chunk in range(5):

            def store(tile, value, chunk=chunk):
                stage[chunk, slot, :, 128 * tile : 128 * tile + 128] = value

            make(chunk, slot, store)
        return carry

    lax.fori_loop(0, 8, body, 0)


def kernel(
    tokens, stage, stage_dt, conv_x, conv_bc, dt_bias,
    gated, states, steps,
    panel, panel_dt, tok, proj, gated_v, states_v,
    a2a_sem, z_sem, ring_sem, sib_sem, send_sem, t_sem, t_send, h_sem, h_send, own_sem, out_sem,
):
    dp, ten = lax.axis_index("dp"), lax.axis_index("tensor")
    core, x, zh = dp % 2, (dp // 2) % 4, dp // 8
    y, zl = ten // 2, ten % 2

    def dp_of(zh_, x_, core_):
        return (zh_ * 4 + x_) * 2 + core_

    left, right, opposite = (x + 3) % 4, (x + 1) % 4, (x + 2) % 4
    up, down, far = (y + 1) % 4, (y + 3) % 4, (y + 2) % 4
    at_right = (dp_of(zh, right, core), ten)
    at_left = (dp_of(zh, left, core), ten)
    at_zh = (dp_of(1 - zh, x, core), ten)
    at_sib = (dp_of(zh, x, 1 - core), ten)
    at_up = (dp, up * 2 + zl)
    at_down = (dp, down * 2 + zl)
    at_zl = (dp, y * 2 + 1 - zl)
    after, before = ((dp + 1) % 16, ten), ((dp + 15) % 16, ten)

    load_t = pltpu.make_async_copy(tokens, tok.at[pl.ds(HALO + ten * TOK, TOK)], own_sem)
    load_t.start()

    barrier = pltpu.get_barrier_semaphore()
    for step in range(1, 8):
        pl.semaphore_signal(barrier, inc=1, device_id=(dp, (ten + step) % 8), device_id_type=MESH)
    for peer in (at_right, at_left, at_zh, at_sib, after, before):
        pl.semaphore_signal(barrier, inc=1, device_id=peer, device_id_type=MESH)

    def remote(src, dst, send, recv, peer):
        return pltpu.make_async_remote_copy(
            src_ref=src, dst_ref=dst, send_sem=send, recv_sem=recv, device_id=peer, device_id_type=MESH
        )

    def tok_rows(y_, zl_):
        return tok.at[pl.ds(HALO + (y_ * 2 + zl_) * TOK, TOK)]

    def tok_send(src, dst, sem, peer):
        remote(src, dst, t_send, t_sem.at[sem], peer).start()

    def tok_wait(sem, y_, zl_):
        ref = tok_rows(y_, zl_)
        pltpu.make_async_copy(ref, ref, t_sem.at[sem]).wait()

    ZL, L0, R0, L1, R1, O0, O1 = range(7)

    def tok_pair():
        tok_wait(ZL, y, 1 - zl)
        ref = tok_rows(y, 1 - zl)
        tok_send(ref, ref, L1, at_up)
        tok_send(ref, ref, R1, at_down)

    def tok_near():
        tok_wait(L0, down, zl)
        ref = tok_rows(down, zl)
        tok_send(ref, ref, O0, at_up)
        tok_wait(R0, up, zl)

    def tok_next():
        tok_wait(R1, up, 1 - zl)
        ref = tok_rows(up, 1 - zl)
        tok_send(ref, ref, O1, at_down)
        tok_wait(L1, down, 1 - zl)

    def tok_far():
        tok_wait(O0, far, zl)
        tok_wait(O1, far, 1 - zl)

    tail = tok.at[pl.ds(ROWS, HALO)]
    head = tok.at[pl.ds(0, HALO)]

    def halo_send(where):
        @pl.when(jnp.logical_and(where, dp < 15))
        def _():
            remote(tail, head, h_send, h_sem, after).start()

    def halo_wait(where):
        @pl.when(jnp.logical_and(where, dp > 0))
        def _():
            pltpu.make_async_copy(head, head, h_sem).wait()

    @pl.when(dp == 0)
    def _():
        tok[0:HALO, :] = jnp.zeros((HALO, D), jnp.bfloat16)

    def rows_of(chunk, start, size):
        return panel_dt.at[pl.ds(start, size)] if chunk == "dt" else panel.at[chunk, pl.ds(start, size)]

    def sem_of(chunk):
        return 5 if chunk == "dt" else chunk

    def block(chunk, zh_, x_, core_):
        return rows_of(chunk, dp_of(zh_, x_, core_) * KB, KB)

    def prepare(chunk):
        mine = dp * KB + ten * KR
        dst = rows_of(chunk, mine, KR)
        sem = a2a_sem.at[sem_of(chunk)]

        def source(slot):
            return stage_dt.at[slot] if chunk == "dt" else stage.at[chunk, slot]

        for step in range(1, 8):
            slot = (ten + step) % 8
            remote(source(slot), dst, send_sem.at[sem_of(chunk)], sem, (dp, slot)).start()
        pltpu.make_async_copy(source(ten), dst, sem).start()

    def send(chunk, ref, recv, peer):
        remote(ref, ref, send_sem.at[sem_of(chunk)], recv.at[sem_of(chunk)], peer).start()

    def wait(chunk, ref, sem):
        pltpu.make_async_copy(ref, ref, sem.at[sem_of(chunk)]).wait()

    def ring(kind):
        return ring_sem.at[kind]

    RL0, RR0, RL1, RR1, RO0, RO1 = range(6)

    def s_own(chunk):
        ref = block(chunk, zh, x, core)
        wait(chunk, ref, a2a_sem)
        send(chunk, ref, z_sem, at_zh)
        send(chunk, ref, ring(RL0), at_right)
        send(chunk, ref, ring(RR0), at_left)
        send(chunk, ref, sib_sem, at_sib)

    def s_pair(chunk):
        ref = block(chunk, 1 - zh, x, core)
        wait(chunk, ref, z_sem)
        send(chunk, ref, ring(RL1), at_right)
        send(chunk, ref, ring(RR1), at_left)
        send(chunk, ref, sib_sem, at_sib)

    def s_near(chunk):
        ref = block(chunk, zh, left, core)
        wait(chunk, ref, ring(RL0))
        send(chunk, ref, ring(RO0), at_right)
        send(chunk, ref, sib_sem, at_sib)
        ref = block(chunk, zh, right, core)
        wait(chunk, ref, ring(RR0))
        send(chunk, ref, sib_sem, at_sib)

    def s_next(chunk):
        ref = block(chunk, 1 - zh, right, core)
        wait(chunk, ref, ring(RR1))
        send(chunk, ref, ring(RO1), at_left)
        send(chunk, ref, sib_sem, at_sib)
        ref = block(chunk, 1 - zh, left, core)
        wait(chunk, ref, ring(RL1))
        send(chunk, ref, sib_sem, at_sib)

    def s_far(chunk):
        ref = block(chunk, zh, opposite, core)
        wait(chunk, ref, ring(RO0))
        send(chunk, ref, sib_sem, at_sib)
        ref = block(chunk, 1 - zh, opposite, core)
        wait(chunk, ref, ring(RO1))
        send(chunk, ref, sib_sem, at_sib)

    def s_sib(chunk):
        wait(chunk, rows_of(chunk, 0, 8 * KB), sib_sem)

    def silu(v):
        return 0.5 * v * (1.0 + jnp.tanh(0.5 * v))

    def rounded(v):
        return v.astype(jnp.bfloat16).astype(jnp.float32)

    def conv(taps, col):
        total = taps[0:1, :] * proj[pl.ds(HALO - 3, GRP), col : col + 256]
        for k in range(1, 4):
            total = total + taps[k : k + 1, :] * proj[pl.ds(HALO - 3 + k, GRP), col : col + 256]
        return total

    def multiply(group, chunk):
        start = pl.multiple_of(group * GRP, GRP)
        lhs = tok[pl.ds(start, HALO + GRP), :]
        for half in range(2):
            cols = slice(256 * half, 256 * half + 256)
            proj[:, cols] = rounded(jnp.dot(lhs, panel[chunk, :, cols], preferred_element_type=jnp.float32))

    def unit(group, chunk):
        multiply(group, chunk)
        start = pl.multiple_of(group * GRP, GRP)
        if chunk == 4:
            for half in range(2):
                cols = slice(256 * half, 256 * half + 256)
                states_v[pl.ds(start, GRP), cols] = silu(conv(conv_bc[:, cols], 256 * half)).astype(jnp.bfloat16)
            src = states_v.at[pl.ds(start, GRP)]
            dst = states.at[pl.ds(start, GRP)]
        else:
            cols = slice(256 * chunk, 256 * chunk + 256)
            value = silu(conv(conv_x[:, cols], 256)) * silu(proj[pl.ds(HALO, GRP), 0:256])
            gated_v[pl.ds(start, GRP), cols] = value.astype(jnp.bfloat16)
            src = gated_v.at[pl.ds(start, GRP), cols]
            dst = gated.at[pl.ds(start, GRP), cols]
        pltpu.make_async_copy(src, dst, out_sem).start()

    def unit_dt(group):
        start = pl.multiple_of(group * GRP, GRP)
        raw = rounded(jnp.dot(tok[pl.ds(start + HALO, GRP), :], panel_dt[...], preferred_element_type=jnp.float32))
        value = raw[:, :HPG] + dt_bias[...]
        steps[pl.ds(start, GRP), :] = jnp.maximum(value, 0.0) + jnp.log1p(jnp.exp(-jnp.abs(value)))

    def units(first, count, chunk):
        def body(step, carry):
            group = (y + first + step) % 4
            if chunk == "dt":
                unit_dt(group)
            else:
                unit(group, chunk)
            return carry

        lax.fori_loop(0, count, body, 0)

    pl.semaphore_wait(barrier, 13)
    own_t = tok_rows(y, zl)
    tok_send(tokens, own_t, ZL, at_zl)
    tok_send(tokens, own_t, L0, at_up)
    tok_send(tokens, own_t, R0, at_down)
    prepare("dt")
    prepare(0)
    s_own("dt")
    prepare(1)
    for k, chunk in enumerate(ORDER):
        s_pair(chunk)
        s_near(chunk)
        if k + 3 < 6:
            prepare(ORDER[k + 3])
        if k + 1 < 6:
            s_own(ORDER[k + 1])
        if k == 3:
            tok_next()
            halo_send(jnp.logical_or(y == 0, y == 2))
        s_next(chunk)
        if k >= 1:
            s_far(ORDER[k - 1])
            s_sib(ORDER[k - 1])
        if k == 1:
            tok_pair()
            tok_near()
            load_t.wait()
            halo_send(y == 3)
        if k == 3:
            halo_wait(jnp.logical_or(y == 0, y == 3))
            units(0, 2, 0)
            units(0, 2, 1)
        if k == 4:
            units(0, 2, 2)
        if k == 5:
            tok_far()
            halo_send(y == 1)
            units(0, 4, "dt")
            halo_wait(jnp.logical_or(y == 1, y == 2))
            for done in range(3):
                units(2, 2, done)
            units(0, 4, 3)
    s_far(4)
    s_sib(4)
    units(0, 4, 4)

    pltpu.make_async_copy(gated_v, gated, out_sem).wait()
    pltpu.make_async_copy(states_v, states, out_sem).wait()
    pltpu.make_async_copy(tok.at[pl.ds(0, 7 * TOK)], tok.at[pl.ds(0, 7 * TOK)], t_send).wait()

    @pl.when(dp < 15)
    def _():
        pltpu.make_async_copy(tail, tail, h_send).wait()

    for chunk in ORDER:
        ref = rows_of(chunk, 0, 15 * KB + 7 * KR)
        wait(chunk, ref, send_sem)


def on_device(tokens, in_weight, group_order, head_order, conv_x, conv_bc, dt_bias):
    vmem, smem, anywhere = (
        pl.BlockSpec(memory_space=pltpu.VMEM),
        pl.BlockSpec(memory_space=pltpu.SMEM),
        pl.BlockSpec(memory_space=pl.ANY),
    )
    dma = pltpu.SemaphoreType.DMA
    bf16, f32 = jnp.bfloat16, jnp.float32
    stage, stage_dt = pl.pallas_call(
        arrange,
        out_shape=(
            jax.ShapeDtypeStruct((5, 8, KR, CW), bf16),
            jax.ShapeDtypeStruct((8, KR, 128), bf16),
        ),
        in_specs=[smem, smem, vmem],
        out_specs=(vmem, vmem),
        scratch_shapes=[pltpu.VMEM((KR, 2688), f32)],
        compiler_params=pltpu.CompilerParams(vmem_limit_bytes=32 << 20),
        cost_estimate=pl.CostEstimate(flops=1 << 20, bytes_accessed=3 << 20, transcendentals=0),
    )(group_order, head_order, in_weight)
    return pl.pallas_call(
        kernel,
        out_shape=(
            jax.ShapeDtypeStruct((ROWS, HPG * HEAD), bf16),
            jax.ShapeDtypeStruct((ROWS, 2 * N), bf16),
            jax.ShapeDtypeStruct((ROWS, HPG), f32),
        ),
        in_specs=[anywhere, anywhere, anywhere, vmem, vmem, vmem],
        out_specs=(anywhere, anywhere, vmem),
        scratch_shapes=[
            pltpu.VMEM((5, D, CW), bf16),
            pltpu.VMEM((D, 128), bf16),
            pltpu.VMEM((HALO + ROWS, D), bf16),
            pltpu.VMEM((HALO + GRP, CW), f32),
            pltpu.VMEM((ROWS, HPG * HEAD), bf16),
            pltpu.VMEM((ROWS, 2 * N), bf16),
            dma((6,)), dma((6,)), dma((6, 6)), dma((6,)), dma((6,)), dma((7,)), dma, dma, dma, dma, dma,
        ],
        compiler_params=pltpu.CompilerParams(
            collective_id=0, has_side_effects=True, vmem_limit_bytes=56 << 20
        ),
        cost_estimate=pl.CostEstimate(
            flops=2 * ROWS * D * GW, bytes_accessed=6 << 20, transcendentals=ROWS * GW
        ),
    )(tokens, stage, stage_dt, conv_x, conv_bc, dt_bias.reshape(1, HPG))


def solution(mesh):
    return jax.shard_map(
        on_device,
        mesh=mesh,
        in_specs=(
            P(("dp", "tensor"), None),
            P(("dp", "tensor"), None),
            P(),
            P(),
            P(None, "tensor"),
            P(None, "tensor"),
            P("tensor"),
        ),
        out_specs=(P("dp", "tensor"), P("dp", "tensor"), P("dp", "tensor")),
        check_vma=False,
    )
```

```python
import functools

import jax
import jax.numpy as jnp
from jax import lax
from jax.experimental import pallas as pl
from jax.experimental.pallas import tpu as pltpu
from jax.sharding import PartitionSpec as P

MESH = pl.DeviceIdType.MESH
HEAD = 64
HPG = 16
N = 256
GW = 2 * HPG * HEAD + 2 * N + HPG
D = 4096
ROWS = 1024
TOK = 128
PIECES = 4
PIECE = TOK // PIECES
HALF = {"b": slice(0, 256), "c": slice(256, 512)}
KB = 256
KR = 32
GRP = 256
HALO = 16
CW = 512
ORDER = ("dt", 0, 1, 2, 3, "b", "c")


def arrange(group_order, head_order, weight, stage, stage_dt, held, lined, sems):
    def fetch(slot):
        start = pl.multiple_of(20 * 128 * group_order[slot], 128)
        return pltpu.make_async_copy(weight.at[:, pl.ds(start, 2688)], held.at[slot], sems.at[slot])

    for slot in range(8):
        fetch(slot).start()

    lane = lax.broadcasted_iota(jnp.int32, (KR, 128), 1)

    def line_up(slot):
        group = group_order[slot]
        fetch(slot).wait()
        for part in range(4):
            wide = held[slot, :, 640 * part : 640 * part + 768].astype(jnp.float32)
            lined[:, 640 * part : 640 * part + 640] = pltpu.roll(wide, (768 - 16 * group) % 768, 1)[:, :640]
        tile = pltpu.roll(held[slot, :, 2560:2688].astype(jnp.float32), (128 - 16 * group) % 128, 1)
        lined[:, 2560:2688] = jnp.where(lane < HPG, tile, 0.0)

    def head_tile(slot, base, first):
        parts = []
        for half in range(2):
            picked = head_order[slot, first + half]
            start = pl.multiple_of(base + 128 * (picked >> 1), 128)
            tile = lined[:, pl.ds(start, 128)]
            parts.append(jnp.where((picked & 1) == half, tile, pltpu.roll(tile, HEAD, 1)))
        return jnp.where(lane < HEAD, parts[0], parts[1]).astype(jnp.bfloat16)

    def make(chunk, slot, store):
        if chunk == "dt":
            source = jnp.full((128, 128), 128, jnp.int32)
            across = lax.broadcasted_iota(jnp.int32, (128, 128), 1)
            for j in range(HPG):
                source = jnp.where(across == j, head_order[slot, j], source)
            down = lax.broadcasted_iota(jnp.int32, (128, 128), 0)
            pick = (down == source).astype(jnp.float32).astype(jnp.bfloat16)
            tile = lined[:, 2560:2688].astype(jnp.bfloat16)
            store(0, jnp.dot(tile, pick, preferred_element_type=jnp.float32).astype(jnp.bfloat16))
        elif chunk == 4:
            for tile in range(4):
                store(tile, lined[:, 2048 + 128 * tile : 2176 + 128 * tile].astype(jnp.bfloat16))
        else:
            for part in range(2):
                for pair in range(2):
                    store(2 * part + pair, head_tile(slot, 1024 * part, 4 * chunk + 2 * pair))

    def body(slot, carry):
        line_up(slot)

        def store_dt(tile, value):
            stage_dt[slot] = value

        make("dt", slot, store_dt)
        for chunk in range(5):

            def store(tile, value, chunk=chunk):
                stage[chunk, slot, :, 128 * tile : 128 * tile + 128] = value

            make(chunk, slot, store)
        return carry

    lax.fori_loop(0, 8, body, 0)


def kernel(
    tokens, stage, stage_dt, conv_x, conv_bc, dt_bias,
    gated, states, steps,
    panel, panel_dt, tok, proj,
    a2a_sem, z_sem, ring_sem, sib_sem, send_sem, t_sem, t_send, h_sem, h_send, own_sem,
):
    dp, ten = lax.axis_index("dp"), lax.axis_index("tensor")
    core, x, zh = dp % 2, (dp // 2) % 4, dp // 8
    y, zl = ten // 2, ten % 2

    def dp_of(zh_, x_, core_):
        return (zh_ * 4 + x_) * 2 + core_

    left, right, opposite = (x + 3) % 4, (x + 1) % 4, (x + 2) % 4
    up, down, far = (y + 1) % 4, (y + 3) % 4, (y + 2) % 4
    at_right = (dp_of(zh, right, core), ten)
    at_left = (dp_of(zh, left, core), ten)
    at_zh = (dp_of(1 - zh, x, core), ten)
    at_sib = (dp_of(zh, x, 1 - core), ten)
    at_up = (dp, up * 2 + zl)
    at_down = (dp, down * 2 + zl)
    at_zl = (dp, y * 2 + 1 - zl)
    after, before = ((dp + 1) % 16, ten), ((dp + 15) % 16, ten)

    load_t = pltpu.make_async_copy(tokens, tok.at[pl.ds(HALO + ten * TOK, TOK)], own_sem)
    load_t.start()

    barrier = pltpu.get_barrier_semaphore()
    for step in range(1, 8):
        pl.semaphore_signal(barrier, inc=1, device_id=(dp, (ten + step) % 8), device_id_type=MESH)
    for peer in (at_right, at_left, at_zh, at_sib, after, before):
        pl.semaphore_signal(barrier, inc=1, device_id=peer, device_id_type=MESH)

    def remote(src, dst, send, recv, peer):
        return pltpu.make_async_remote_copy(
            src_ref=src, dst_ref=dst, send_sem=send, recv_sem=recv, device_id=peer, device_id_type=MESH
        )

    def tok_rows(y_, zl_, piece):
        return tok.at[pl.ds(HALO + (y_ * 2 + zl_) * TOK + piece * PIECE, PIECE)]

    ZL, L0, R0, L1, R1, O0, O1 = range(7)
    arrives = {
        ZL: (y, 1 - zl), L0: (down, zl), R0: (up, zl), L1: (down, 1 - zl),
        R1: (up, 1 - zl), O0: (far, zl), O1: (far, 1 - zl),
    }
    waited = set()

    def tok_wait(*kinds, pieces=range(PIECES)):
        for kind in kinds:
            for piece in pieces:
                if (kind, piece) not in waited:
                    waited.add((kind, piece))
                    ref = tok_rows(*arrives[kind], piece)
                    pltpu.make_async_copy(ref, ref, t_sem.at[kind, piece]).wait()

    def tok_send(ref, dst, kind, piece, peer):
        remote(ref, dst, t_send, t_sem.at[kind, piece], peer).start()

    def slot(q):
        piece = PIECES - 1 - q % PIECES
        if q < PIECES:
            src, dst = tokens.at[pl.ds(piece * PIECE, PIECE)], tok_rows(y, zl, piece)
            tok_send(src, dst, L0, piece, at_up)
            tok_send(src, dst, R0, piece, at_down)
        elif q < 2 * PIECES:
            tok_wait(ZL, pieces=(piece,))
            ref = tok_rows(y, 1 - zl, piece)
            tok_send(ref, ref, L1, piece, at_up)
            tok_send(ref, ref, R1, piece, at_down)
        else:
            tok_wait(L0, R1, pieces=(piece,))
            ref = tok_rows(down, zl, piece)
            tok_send(ref, ref, O0, piece, at_up)
            ref = tok_rows(up, 1 - zl, piece)
            tok_send(ref, ref, O1, piece, at_down)

    def across(piece):
        src, dst = tokens.at[pl.ds(piece * PIECE, PIECE)], tok_rows(y, zl, piece)
        tok_send(src, dst, ZL, piece, at_zl)

    def tok_near():
        tok_wait(ZL, L0, R0, L1, R1)

    def tok_far():
        tok_wait(O0, O1)

    tail = tok.at[pl.ds(ROWS, HALO)]
    head = tok.at[pl.ds(0, HALO)]

    def halo_send(where):
        @pl.when(jnp.logical_and(where, dp < 15))
        def _():
            remote(tail, head, h_send, h_sem, after).start()

    def halo_wait(where):
        @pl.when(jnp.logical_and(where, dp > 0))
        def _():
            pltpu.make_async_copy(head, head, h_sem).wait()

    @pl.when(dp == 0)
    def _():
        tok[0:HALO, :] = jnp.zeros((HALO, D), jnp.bfloat16)

    def rows_of(chunk, start, size):
        if chunk == "dt":
            return panel_dt.at[pl.ds(start, size)]
        if chunk in ("b", "c"):
            return panel.at[4, pl.ds(start, size), HALF[chunk]]
        return panel.at[chunk, pl.ds(start, size)]

    def sem_of(chunk):
        return ORDER.index(chunk)

    def block(chunk, zh_, x_, core_):
        return rows_of(chunk, dp_of(zh_, x_, core_) * KB, KB)

    def prepare(chunk):
        mine = dp * KB + ten * KR
        dst = rows_of(chunk, mine, KR)
        sem = a2a_sem.at[sem_of(chunk)]

        def source(slot):
            if chunk == "dt":
                return stage_dt.at[slot]
            if chunk in ("b", "c"):
                return stage.at[4, slot, :, HALF[chunk]]
            return stage.at[chunk, slot]

        for step in range(1, 8):
            slot = (ten + step) % 8
            remote(source(slot), dst, send_sem.at[sem_of(chunk)], sem, (dp, slot)).start()
        pltpu.make_async_copy(source(ten), dst, sem).start()

    def send(chunk, ref, recv, peer):
        remote(ref, ref, send_sem.at[sem_of(chunk)], recv.at[sem_of(chunk)], peer).start()

    def wait(chunk, ref, sem):
        pltpu.make_async_copy(ref, ref, sem.at[sem_of(chunk)]).wait()

    def ring(kind):
        return ring_sem.at[kind]

    RL0, RR0, RL1, RR1, RO0, RO1 = range(6)

    def s_own(chunk):
        ref = block(chunk, zh, x, core)
        wait(chunk, ref, a2a_sem)
        send(chunk, ref, z_sem, at_zh)
        send(chunk, ref, ring(RL0), at_right)
        send(chunk, ref, ring(RR0), at_left)
        send(chunk, ref, sib_sem, at_sib)

    def s_pair(chunk):
        ref = block(chunk, 1 - zh, x, core)
        wait(chunk, ref, z_sem)
        send(chunk, ref, ring(RL1), at_right)
        send(chunk, ref, ring(RR1), at_left)
        send(chunk, ref, sib_sem, at_sib)

    def s_near(chunk):
        ref = block(chunk, zh, left, core)
        wait(chunk, ref, ring(RL0))
        send(chunk, ref, ring(RO0), at_right)
        send(chunk, ref, sib_sem, at_sib)
        ref = block(chunk, zh, right, core)
        wait(chunk, ref, ring(RR0))
        send(chunk, ref, sib_sem, at_sib)

    def s_next(chunk):
        ref = block(chunk, 1 - zh, right, core)
        wait(chunk, ref, ring(RR1))
        send(chunk, ref, ring(RO1), at_left)
        send(chunk, ref, sib_sem, at_sib)
        ref = block(chunk, 1 - zh, left, core)
        wait(chunk, ref, ring(RL1))
        send(chunk, ref, sib_sem, at_sib)

    def s_far(chunk):
        ref = block(chunk, zh, opposite, core)
        wait(chunk, ref, ring(RO0))
        send(chunk, ref, sib_sem, at_sib)
        ref = block(chunk, 1 - zh, opposite, core)
        wait(chunk, ref, ring(RO1))
        send(chunk, ref, sib_sem, at_sib)

    def s_sib(chunk):
        wait(chunk, rows_of(chunk, 0, 8 * KB), sib_sem)

    def silu(v):
        return 0.5 * v * (1.0 + jnp.tanh(0.5 * v))

    def rounded(v):
        return v.astype(jnp.bfloat16).astype(jnp.float32)

    def conv(taps, col):
        total = taps[0:1, :] * proj[pl.ds(HALO - 3, GRP), col : col + 256]
        for k in range(1, 4):
            total = total + taps[k : k + 1, :] * proj[pl.ds(HALO - 3 + k, GRP), col : col + 256]
        return total

    def unit(group, chunk):
        start = pl.multiple_of(group * GRP, GRP)
        lhs = tok[pl.ds(start, HALO + GRP), :]
        if chunk in ("b", "c"):
            cols = HALF[chunk]
            proj[:, 256:512] = rounded(jnp.dot(lhs, panel[4, :, cols], preferred_element_type=jnp.float32))
            states[pl.ds(start, GRP), cols] = silu(conv(conv_bc[:, cols], 256)).astype(jnp.bfloat16)
        else:
            for half in HALF.values():
                proj[:, half] = rounded(jnp.dot(lhs, panel[chunk, :, half], preferred_element_type=jnp.float32))
            cols = slice(256 * chunk, 256 * chunk + 256)
            value = silu(conv(conv_x[:, cols], 256)) * silu(proj[pl.ds(HALO, GRP), 0:256])
            gated[pl.ds(start, GRP), cols] = value.astype(jnp.bfloat16)

    def unit_dt(group):
        start = pl.multiple_of(group * GRP, GRP)
        raw = rounded(jnp.dot(tok[pl.ds(start + HALO, GRP), :], panel_dt[...], preferred_element_type=jnp.float32))
        value = (raw[:, :HPG] + dt_bias[...]).T
        steps[:, pl.ds(start, GRP)] = jnp.maximum(value, 0.0) + jnp.log1p(jnp.exp(-jnp.abs(value)))

    def units(places, *chunks):
        def body(step, carry):
            group = groups[places[0]]
            for index, place in enumerate(places[1:]):
                group = jnp.where(step == index + 1, groups[place], group)
            for chunk in chunks:
                if chunk == "dt":
                    unit_dt(group)
                else:
                    unit(group, chunk)
            return carry

        if len(places) == 1:
            body(0, 0)
        else:
            lax.fori_loop(0, len(places), body, 0)

    ends = jnp.logical_or(y == 0, y == 3)
    groups = (
        jnp.where(y == 3, 3, up),
        jnp.where(ends, down, y),
        jnp.where(ends, 0, down),
        far,
    )

    pl.semaphore_wait(barrier, 13)
    prepare("dt")
    prepare(0)
    slot(0)
    s_own("dt")
    s_own(0)
    prepare(1)
    across(3)
    slot(1)
    s_pair("dt")
    s_near("dt")
    across(2)
    slot(2)
    prepare(2)
    s_next("dt")
    s_pair(0)
    s_own(1)
    s_near(0)
    across(1)
    slot(3)
    s_next(0)
    s_far("dt")
    across(0)
    slot(4)
    load_t.wait()
    halo_send(y == 3)
    s_pair(1)
    s_own(2)
    s_near(1)
    slot(5)
    prepare(3)
    s_next(1)
    slot(6)
    s_far(0)
    slot(7)
    prepare("b")
    prepare("c")
    s_pair(2)
    s_own(3)
    s_near(2)
    slot(8)
    tok_wait(R0, L1, pieces=(3,))
    halo_send(jnp.logical_or(y == 0, y == 2))
    s_next(2)
    slot(9)
    s_far(1)
    slot(10)
    tok_wait(L0, R0, L1, R1)
    s_sib("dt")
    s_sib(0)
    units((0,), "dt", 0)
    s_pair(3)
    s_own("b")
    slot(11)
    s_sib(1)
    units((0,), 1)
    s_near(3)
    s_own("c")
    tok_wait(O0, O1, pieces=(3,))
    halo_send(y == 1)
    units((1,), "dt", 0, 1)
    s_next(3)
    s_far(2)
    halo_wait(y != 2)
    units((2,), "dt", 0, 1)
    s_pair("b")
    s_near("b")
    s_sib(2)
    units((0, 1, 2), 2)
    s_next("b")
    s_far(3)
    s_pair("c")
    s_near("c")
    tok_far()
    halo_wait(y == 2)
    units((3,), "dt", 0)
    s_next("c")
    units((3,), 1, 2)
    s_far("b")
    s_sib(3)
    units((0, 1, 2, 3), 3)
    s_far("c")
    s_sib("b")
    units((0, 1, 2, 3), "b")
    s_sib("c")
    units((0, 1, 2, 3), "c")

    pltpu.make_async_copy(tok.at[pl.ds(0, 7 * TOK)], tok.at[pl.ds(0, 7 * TOK)], t_send).wait()

    @pl.when(dp < 15)
    def _():
        pltpu.make_async_copy(tail, tail, h_send).wait()

    for chunk in ORDER:
        ref = rows_of(chunk, 0, 15 * KB + 7 * KR)
        wait(chunk, ref, send_sem)


def finish(gated_v, states_v, steps_v, gated, states, steps, sems):
    copies = [pltpu.make_async_copy(steps_v, steps, sems.at[6])]
    for part in range(4):
        rows = pl.ds(GRP * part, GRP)
        copies.append(pltpu.make_async_copy(gated_v.at[rows], gated.at[rows], sems.at[part]))
    for part in range(2):
        rows = pl.ds(2 * GRP * part, 2 * GRP)
        copies.append(pltpu.make_async_copy(states_v.at[rows], states.at[rows], sems.at[4 + part]))
    for copy in copies:
        copy.start()
    for copy in copies:
        copy.wait()


def on_device(tokens, in_weight, group_order, head_order, conv_x, conv_bc, dt_bias):
    vmem, smem, anywhere = (
        pl.BlockSpec(memory_space=pltpu.VMEM),
        pl.BlockSpec(memory_space=pltpu.SMEM),
        pl.BlockSpec(memory_space=pl.ANY),
    )
    dma = pltpu.SemaphoreType.DMA
    bf16, f32 = jnp.bfloat16, jnp.float32
    def at_vmem(value):
        return pltpu.with_memory_space_constraint(value, pltpu.VMEM)

    def at_hbm(value):
        return pltpu.with_memory_space_constraint(value, pltpu.HBM)

    stage, stage_dt = pl.pallas_call(
        arrange,
        out_shape=(pltpu.VMEM((5, 8, KR, CW), bf16), pltpu.VMEM((8, KR, 128), bf16)),
        in_specs=[smem, smem, anywhere],
        out_specs=(vmem, vmem),
        scratch_shapes=[pltpu.VMEM((8, KR, 2688), bf16), pltpu.VMEM((KR, 2688), f32), dma((8,))],
        compiler_params=pltpu.CompilerParams(vmem_limit_bytes=32 << 20),
        cost_estimate=pl.CostEstimate(flops=1 << 20, bytes_accessed=3 << 20, transcendentals=0),
    )(at_hbm(group_order), at_hbm(head_order), at_hbm(in_weight))
    gated, states, steps = pl.pallas_call(
        kernel,
        out_shape=(
            pltpu.VMEM((ROWS, HPG * HEAD), bf16),
            pltpu.VMEM((ROWS, 2 * N), bf16),
            pltpu.VMEM((HPG, ROWS), f32),
        ),
        in_specs=[anywhere, vmem, vmem, vmem, vmem, vmem],
        out_specs=(vmem, vmem, vmem),
        scratch_shapes=[
            pltpu.VMEM((5, D, CW), bf16),
            pltpu.VMEM((D, 128), bf16),
            pltpu.VMEM((HALO + ROWS, D), bf16),
            pltpu.VMEM((HALO + GRP, CW), f32),
            dma((7,)), dma((7,)), dma((6, 7)), dma((7,)), dma((7,)), dma((7, PIECES)), dma, dma, dma, dma,
        ],
        compiler_params=pltpu.CompilerParams(
            collective_id=0, has_side_effects=True, vmem_limit_bytes=56 << 20
        ),
        cost_estimate=pl.CostEstimate(
            flops=2 * ROWS * D * GW, bytes_accessed=6 << 20, transcendentals=ROWS * GW
        ),
    )(at_hbm(tokens), at_vmem(stage), at_vmem(stage_dt), conv_x, conv_bc, dt_bias.reshape(1, HPG))
    gated, states, steps = pl.pallas_call(
        finish,
        out_shape=(
            pltpu.HBM((ROWS, HPG * HEAD), bf16),
            pltpu.HBM((ROWS, 2 * N), bf16),
            pltpu.HBM((HPG, ROWS), f32),
        ),
        in_specs=[vmem, vmem, vmem],
        out_specs=(anywhere, anywhere, anywhere),
        scratch_shapes=[dma((7,))],
        cost_estimate=pl.CostEstimate(flops=0, bytes_accessed=3 << 20, transcendentals=0),
    )(at_vmem(gated), at_vmem(states), at_vmem(steps))
    return gated, states, steps.T


def solution(mesh):
    return jax.shard_map(
        on_device,
        mesh=mesh,
        in_specs=(
            P(("dp", "tensor"), None),
            P(("dp", "tensor"), None),
            P(),
            P(),
            P(None, "tensor"),
            P(None, "tensor"),
            P("tensor"),
        ),
        out_specs=(P("dp", "tensor"), P("dp", "tensor"), P("dp", "tensor")),
        check_vma=False,
    )
```

```python
import functools

import jax
import jax.numpy as jnp
from jax import lax
from jax.experimental import pallas as pl
from jax.experimental.pallas import tpu as pltpu
from jax.sharding import PartitionSpec as P

MESH = pl.DeviceIdType.MESH
HEAD = 64
HPG = 16
N = 256
GW = 2 * HPG * HEAD + 2 * N + HPG
D = 4096
ROWS = 1024
TOK = 128
PIECES = 4
PIECE = TOK // PIECES
HALF = {"b": slice(0, 256), "c": slice(256, 512)}
KB = 256
KR = 32
GRP = 256
HALO = 16
CW = 512
ORDER = ("dt", 0, 1, 2, 3, "b", "c")
BY_Z = ("b", "c")


def arrange(group_order, head_order, weight, stage, stage_dt, held, lined, sems):
    def fetch(slot):
        start = pl.multiple_of(20 * 128 * group_order[slot], 128)
        return pltpu.make_async_copy(weight.at[:, pl.ds(start, 2688)], held.at[slot], sems.at[slot])

    for slot in range(8):
        fetch(slot).start()

    lane = lax.broadcasted_iota(jnp.int32, (KR, 128), 1)
    ten = lax.axis_index("tensor")

    def line_up(slot):
        group = group_order[slot]
        fetch(slot).wait()
        for part in range(4):
            wide = held[slot, :, 640 * part : 640 * part + 768].astype(jnp.float32)
            lined[:, 640 * part : 640 * part + 640] = pltpu.roll(wide, (768 - 16 * group) % 768, 1)[:, :640]
        tile = pltpu.roll(held[slot, :, 2560:2688].astype(jnp.float32), (128 - 16 * group) % 128, 1)
        lined[:, 2560:2688] = jnp.where(lane < HPG, tile, 0.0)

    def head_tile(slot, base, first):
        parts = []
        for half in range(2):
            picked = head_order[slot, first + half]
            start = pl.multiple_of(base + 128 * (picked >> 1), 128)
            tile = lined[:, pl.ds(start, 128)]
            parts.append(jnp.where((picked & 1) == half, tile, pltpu.roll(tile, HEAD, 1)))
        return jnp.where(lane < HEAD, parts[0], parts[1]).astype(jnp.bfloat16)

    def make(chunk, slot, store):
        if chunk == "dt":
            source = jnp.full((128, 128), 128, jnp.int32)
            across = lax.broadcasted_iota(jnp.int32, (128, 128), 1)
            for j in range(HPG):
                source = jnp.where(across == j + HPG * ten, head_order[slot, j], source)
            down = lax.broadcasted_iota(jnp.int32, (128, 128), 0)
            pick = (down == source).astype(jnp.float32).astype(jnp.bfloat16)
            tile = lined[:, 2560:2688].astype(jnp.bfloat16)
            store(0, jnp.dot(tile, pick, preferred_element_type=jnp.float32).astype(jnp.bfloat16))
        elif chunk == 4:
            for tile in range(4):
                store(tile, lined[:, 2048 + 128 * tile : 2176 + 128 * tile].astype(jnp.bfloat16))
        else:
            for part in range(2):
                for pair in range(2):
                    store(2 * part + pair, head_tile(slot, 1024 * part, 4 * chunk + 2 * pair))

    def body(slot, carry):
        line_up(slot)

        def store_dt(tile, value):
            stage_dt[slot] = value

        make("dt", slot, store_dt)
        for chunk in range(5):

            def store(tile, value, chunk=chunk):
                stage[chunk, slot, :, 128 * tile : 128 * tile + 128] = value

            make(chunk, slot, store)
        return carry

    lax.fori_loop(0, 8, body, 0)


def kernel(
    tokens, stage, stage_dt, conv_x, conv_bc, dt_bias,
    gated, states, steps,
    panel, panel_dt, dt_in, dt_all, tok, proj,
    a2a_sem, z_sem, ring_sem, sib_sem, send_sem, t_sem, t_send, h_sem, h_send, own_sem,
):
    dp, ten = lax.axis_index("dp"), lax.axis_index("tensor")
    core, x, zh = dp % 2, (dp // 2) % 4, dp // 8
    y, zl = ten // 2, ten % 2

    def dp_of(zh_, x_, core_):
        return (zh_ * 4 + x_) * 2 + core_

    left, right, opposite = (x + 3) % 4, (x + 1) % 4, (x + 2) % 4
    up, down, far = (y + 1) % 4, (y + 3) % 4, (y + 2) % 4
    at_right = (dp_of(zh, right, core), ten)
    at_left = (dp_of(zh, left, core), ten)
    at_zh = (dp_of(1 - zh, x, core), ten)
    at_sib = (dp_of(zh, x, 1 - core), ten)
    at_up = (dp, up * 2 + zl)
    at_down = (dp, down * 2 + zl)
    at_zl = (dp, y * 2 + 1 - zl)
    after, before = ((dp + 1) % 16, ten), ((dp + 15) % 16, ten)

    load_t = pltpu.make_async_copy(tokens, tok.at[pl.ds(HALO + ten * TOK, TOK)], own_sem)
    load_t.start()

    barrier = pltpu.get_barrier_semaphore()
    for step in range(1, 8):
        pl.semaphore_signal(barrier, inc=1, device_id=(dp, (ten + step) % 8), device_id_type=MESH)
    for peer in (at_right, at_left, at_zh, at_sib, after, before):
        pl.semaphore_signal(barrier, inc=1, device_id=peer, device_id_type=MESH)

    def remote(src, dst, send, recv, peer):
        return pltpu.make_async_remote_copy(
            src_ref=src, dst_ref=dst, send_sem=send, recv_sem=recv, device_id=peer, device_id_type=MESH
        )

    def tok_rows(y_, zl_, piece):
        return tok.at[pl.ds(HALO + (y_ * 2 + zl_) * TOK + piece * PIECE, PIECE)]

    ZL, L0, R0, L1, R1, O0, O1 = range(7)
    arrives = {
        ZL: (y, 1 - zl), L0: (down, zl), R0: (up, zl), L1: (down, 1 - zl),
        R1: (up, 1 - zl), O0: (far, zl), O1: (far, 1 - zl),
    }
    waited = set()

    def tok_wait(*kinds, pieces=range(PIECES)):
        for kind in kinds:
            for piece in pieces:
                if (kind, piece) not in waited:
                    waited.add((kind, piece))
                    ref = tok_rows(*arrives[kind], piece)
                    pltpu.make_async_copy(ref, ref, t_sem.at[kind, piece]).wait()

    def tok_send(ref, dst, kind, piece, peer):
        remote(ref, dst, t_send, t_sem.at[kind, piece], peer).start()

    def slot(q):
        piece = PIECES - 1 - q % PIECES
        if q < PIECES:
            src, dst = tokens.at[pl.ds(piece * PIECE, PIECE)], tok_rows(y, zl, piece)
            tok_send(src, dst, L0, piece, at_up)
            tok_send(src, dst, R0, piece, at_down)
        elif q < 2 * PIECES:
            tok_wait(ZL, pieces=(piece,))
            ref = tok_rows(y, 1 - zl, piece)
            tok_send(ref, ref, L1, piece, at_up)
            tok_send(ref, ref, R1, piece, at_down)
        else:
            tok_wait(L0, R1, pieces=(piece,))
            ref = tok_rows(down, zl, piece)
            tok_send(ref, ref, O0, piece, at_up)
            ref = tok_rows(up, 1 - zl, piece)
            tok_send(ref, ref, O1, piece, at_down)

    def across(piece):
        src, dst = tokens.at[pl.ds(piece * PIECE, PIECE)], tok_rows(y, zl, piece)
        tok_send(src, dst, ZL, piece, at_zl)

    def tok_near():
        tok_wait(ZL, L0, R0, L1, R1)

    def tok_far():
        tok_wait(O0, O1)

    head = tok.at[pl.ds(0, HALO)]

    def halo_send(where, src, *peers):
        @pl.when(where)
        def _():
            for peer in peers:
                remote(src, head, h_send, h_sem, peer).start()

    def halo_wait(where):
        @pl.when(jnp.logical_and(where, dp > 0))
        def _():
            pltpu.make_async_copy(head, head, h_sem).wait()

    def halo_sent(where, count):
        @pl.when(where)
        def _():
            for _ in range(count):
                pltpu.make_async_copy(head, head, h_send).wait()

    halo_first = jnp.logical_and(ten == 7, dp < 15)
    halo_a = ten == 7
    halo_b = ten == 6
    halo_c = ten == 1
    halo_d = ten == 4
    halo_rest = jnp.logical_or(jnp.logical_or(ten == 0, ten == 5), y == 1)
    inner = dp > 0

    @pl.when(dp == 0)
    def _():
        tok[0:HALO, :] = jnp.zeros((HALO, D), jnp.bfloat16)

    def rows_of(chunk, start, size):
        if chunk == "dt":
            return dt_all.at[pl.ds(start, size)]
        if chunk in ("b", "c"):
            return panel.at[4, pl.ds(start, size), HALF[chunk]]
        return panel.at[chunk, pl.ds(start, size)]

    def sem_of(chunk):
        return ORDER.index(chunk)

    def height(chunk):
        return KR if chunk == "dt" else KB

    def block(chunk, zh_, x_, core_):
        return rows_of(chunk, dp_of(zh_, x_, core_) * height(chunk), height(chunk))

    def prepare(chunk):
        if chunk == "dt":
            dst, sent = dt_in.at[pl.ds(ten * KR, KR)], send_sem.at[len(ORDER)]
        else:
            dst, sent = rows_of(chunk, dp * KB + ten * KR, KR), send_sem.at[sem_of(chunk)]
        sem = a2a_sem.at[sem_of(chunk)]

        def source(slot):
            if chunk == "dt":
                return stage_dt.at[slot]
            if chunk in ("b", "c"):
                return stage.at[4, slot, :, HALF[chunk]]
            return stage.at[chunk, slot]

        for step in range(1, 8):
            slot = (ten + step) % 8
            remote(source(slot), dst, sent, sem, (dp, slot)).start()
        pltpu.make_async_copy(source(ten), dst, sem).start()

    def send(chunk, ref, recv, peer):
        remote(ref, ref, send_sem.at[sem_of(chunk)], recv.at[sem_of(chunk)], peer).start()

    def wait(chunk, ref, sem):
        pltpu.make_async_copy(ref, ref, sem.at[sem_of(chunk)]).wait()

    def ring(kind):
        return ring_sem.at[kind]

    RL0, RR0, RL1, RR1, RO0, RO1 = range(6)

    def s_z(chunk):
        send(chunk, block(chunk, zh, x, core), z_sem, at_zh)

    def s_ready(chunk):
        if chunk == "dt":
            pltpu.make_async_copy(dt_in, dt_in, a2a_sem.at[sem_of(chunk)]).wait()
            total = dt_in[0:KR, :].astype(jnp.float32)
            for sender in range(1, 8):
                total = total + dt_in[KR * sender : KR * sender + KR, :].astype(jnp.float32)
            dt_all[pl.ds(dp * KR, KR), :] = total.astype(jnp.bfloat16)
        else:
            wait(chunk, block(chunk, zh, x, core), a2a_sem)

    def s_own(chunk):
        ref = block(chunk, zh, x, core)
        send(chunk, ref, ring(RL0), at_right)
        send(chunk, ref, ring(RR0), at_left)
        send(chunk, ref, sib_sem, at_sib)

    def s_pair(chunk):
        ref = block(chunk, 1 - zh, x, core)
        wait(chunk, ref, z_sem)
        if chunk not in BY_Z:
            send(chunk, ref, ring(RL1), at_right)
            send(chunk, ref, ring(RR1), at_left)
        send(chunk, ref, sib_sem, at_sib)

    def s_near(chunk):
        ref = block(chunk, zh, left, core)
        wait(chunk, ref, ring(RL0))
        send(chunk, ref, ring(RO0), at_right)
        if chunk in BY_Z:
            send(chunk, ref, ring(RL1), at_zh)
        send(chunk, ref, sib_sem, at_sib)
        ref = block(chunk, zh, right, core)
        wait(chunk, ref, ring(RR0))
        if chunk in BY_Z:
            send(chunk, ref, ring(RR1), at_zh)
        send(chunk, ref, sib_sem, at_sib)

    def s_next(chunk):
        ref = block(chunk, 1 - zh, right, core)
        wait(chunk, ref, ring(RR1))
        send(chunk, ref, ring(RO1), at_left)
        send(chunk, ref, sib_sem, at_sib)
        ref = block(chunk, 1 - zh, left, core)
        wait(chunk, ref, ring(RL1))
        send(chunk, ref, sib_sem, at_sib)

    def s_far(chunk):
        ref = block(chunk, zh, opposite, core)
        wait(chunk, ref, ring(RO0))
        send(chunk, ref, sib_sem, at_sib)
        ref = block(chunk, 1 - zh, opposite, core)
        wait(chunk, ref, ring(RO1))
        send(chunk, ref, sib_sem, at_sib)

    def s_sib(chunk):
        wait(chunk, rows_of(chunk, 0, 8 * height(chunk)), sib_sem)

    def unpack():
        packed = dt_all[...].astype(jnp.float32)
        for sender in range(8):
            turned = pltpu.roll(packed, (128 - HPG * sender) % 128, 1)
            panel_dt[:, sender] = turned.reshape(16, KR, 128).astype(jnp.bfloat16)

    def silu(v):
        return 0.5 * v * (1.0 + jnp.tanh(0.5 * v))

    def rounded(v):
        return v.astype(jnp.bfloat16).astype(jnp.float32)

    def conv(taps, size, col):
        total = taps[0:1, :] * proj[pl.ds(HALO - 3, size), col : col + 256]
        for k in range(1, 4):
            total = total + taps[k : k + 1, :] * proj[pl.ds(HALO - 3 + k, size), col : col + 256]
        return total

    def unit(start, size, chunk):
        lhs = tok[pl.ds(start, HALO + size), :]
        into = pl.ds(0, HALO + size)
        if chunk in ("b", "c"):
            cols = HALF[chunk]
            proj[into, 256:512] = rounded(jnp.dot(lhs, panel[4, :, cols], preferred_element_type=jnp.float32))
            states[pl.ds(start, size), cols] = silu(conv(conv_bc[:, cols], size, 256)).astype(jnp.bfloat16)
        else:
            for half in HALF.values():
                proj[into, half] = rounded(jnp.dot(lhs, panel[chunk, :, half], preferred_element_type=jnp.float32))
            cols = slice(256 * chunk, 256 * chunk + 256)
            value = silu(conv(conv_x[:, cols], size, 256)) * silu(proj[pl.ds(HALO, size), 0:256])
            gated[pl.ds(start, size), cols] = value.astype(jnp.bfloat16)

    def whole(chunk):
        def body(step, carry):
            unit(pl.multiple_of(step * 2 * GRP, 2 * GRP), 2 * GRP, chunk)
            return carry

        lax.fori_loop(0, 2, body, 0)

    def unit_dt(group):
        start = pl.multiple_of(group * GRP, GRP)
        raw = rounded(jnp.dot(tok[pl.ds(start + HALO, GRP), :], panel_dt[...].reshape(D, 128), preferred_element_type=jnp.float32))
        value = (raw[:, :HPG] + dt_bias[...]).T
        steps[:, pl.ds(start, GRP)] = jnp.maximum(value, 0.0) + jnp.log1p(jnp.exp(-jnp.abs(value)))

    def units(places, *chunks):
        def body(step, carry):
            group = groups[places[0]]
            for index, place in enumerate(places[1:]):
                group = jnp.where(step == index + 1, groups[place], group)
            for chunk in chunks:
                if chunk == "dt":
                    unit_dt(group)
                else:
                    unit(pl.multiple_of(group * GRP, GRP), GRP, chunk)
            return carry

        if len(places) == 1:
            body(0, 0)
        else:
            lax.fori_loop(0, len(places), body, 0)

    groups = (y, up, down, far)

    pl.semaphore_wait(barrier, 13)
    prepare(0)
    halo_send(halo_first, tokens.at[pl.ds(TOK - HALO, HALO)], after)
    prepare(1)
    prepare("dt")
    s_ready(0)
    s_z(0)
    s_own(0)
    prepare(2)
    slot(0)
    s_ready(1)
    s_own(1)
    s_near(0)
    across(3)
    slot(1)
    halo_wait(halo_a)
    halo_send(jnp.logical_and(halo_a, inner), head, at_zl, at_up, at_down)
    s_pair(0)
    s_z(1)
    s_ready("dt")
    s_z("dt")
    s_own("dt")
    s_ready(2)
    s_own(2)
    prepare(3)
    slot(2)
    across(2)
    s_next(0)
    s_near(1)
    across(1)
    slot(3)
    halo_wait(halo_b)
    halo_send(jnp.logical_and(halo_b, inner), head, at_up, at_down)
    s_pair(1)
    s_z(2)
    slot(4)
    prepare("b")
    s_near("dt")
    s_pair("dt")
    s_ready(3)
    s_own(3)
    slot(5)
    across(0)
    s_next(1)
    s_near(2)
    s_far(0)
    slot(6)
    prepare("c")
    s_pair(2)
    s_z(3)
    halo_wait(jnp.logical_or(halo_c, halo_d))
    halo_send(jnp.logical_and(halo_c, inner), head, at_up)
    halo_send(jnp.logical_and(halo_d, inner), head, at_down)
    s_ready("b")
    s_own("b")
    slot(7)
    s_next("dt")
    load_t.wait()
    halo_wait(halo_rest)
    tok_wait(ZL)
    tok_wait(L0, L1, pieces=(3,))
    s_sib(0)
    units((0,), 0)
    slot(8)
    s_next(2)
    s_near(3)
    s_pair(3)
    s_z("b")
    s_far(1)
    s_ready("c")
    s_own("c")
    slot(9)
    s_sib(1)
    units((0,), 1)
    s_far("dt")
    s_sib("dt")
    unpack()
    units((0,), "dt")
    slot(10)
    tok_wait(L0, R0, L1, R1)
    units((1,), "dt", 0, 1)
    slot(11)
    tok_wait(O0, O1, pieces=(3,))
    units((2,), 0)
    s_next(3)
    s_near("b")
    s_pair("b")
    s_z("c")
    s_far(2)
    s_sib(2)
    units((0, 1), 2)
    s_next("b")
    s_near("c")
    s_pair("c")
    units((2,), "dt", 1, 2)
    s_far(3)
    s_next("c")
    s_far("b")
    s_sib(3)
    units((0, 1), 3)
    s_far("c")
    units((2,), 3)
    tok_far()
    units((3,), "dt", 0, 1)
    units((3,), 2, 3)
    s_sib("b")
    whole("b")
    s_sib("c")
    whole("c")

    pltpu.make_async_copy(tok.at[pl.ds(0, 7 * TOK)], tok.at[pl.ds(0, 7 * TOK)], t_send).wait()

    halo_sent(halo_first, 1)
    halo_sent(jnp.logical_and(halo_a, inner), 3)
    halo_sent(jnp.logical_and(halo_b, inner), 2)
    halo_sent(jnp.logical_and(jnp.logical_or(halo_c, halo_d), inner), 1)

    for chunk in ORDER[1:]:
        wait(chunk, rows_of(chunk, 0, 15 * KB + 7 * KR), send_sem)
    wait("dt", rows_of("dt", 0, 15 * KR), send_sem)
    ref = dt_in.at[pl.ds(0, 7 * KR)]
    pltpu.make_async_copy(ref, ref, send_sem.at[len(ORDER)]).wait()


def finish(gated_v, states_v, steps_v, gated, states, steps, sems):
    copies = [pltpu.make_async_copy(steps_v, steps, sems.at[6])]
    for part in range(4):
        rows = pl.ds(GRP * part, GRP)
        copies.append(pltpu.make_async_copy(gated_v.at[rows], gated.at[rows], sems.at[part]))
    for part in range(2):
        rows = pl.ds(2 * GRP * part, 2 * GRP)
        copies.append(pltpu.make_async_copy(states_v.at[rows], states.at[rows], sems.at[4 + part]))
    for copy in copies:
        copy.start()
    for copy in copies:
        copy.wait()


def on_device(tokens, in_weight, group_order, head_order, conv_x, conv_bc, dt_bias):
    vmem, smem, anywhere = (
        pl.BlockSpec(memory_space=pltpu.VMEM),
        pl.BlockSpec(memory_space=pltpu.SMEM),
        pl.BlockSpec(memory_space=pl.ANY),
    )
    dma = pltpu.SemaphoreType.DMA
    bf16, f32 = jnp.bfloat16, jnp.float32
    def at_vmem(value):
        return pltpu.with_memory_space_constraint(value, pltpu.VMEM)

    def at_hbm(value):
        return pltpu.with_memory_space_constraint(value, pltpu.HBM)

    stage, stage_dt = pl.pallas_call(
        arrange,
        out_shape=(pltpu.VMEM((5, 8, KR, CW), bf16), pltpu.VMEM((8, KR, 128), bf16)),
        in_specs=[smem, smem, anywhere],
        out_specs=(vmem, vmem),
        scratch_shapes=[pltpu.VMEM((8, KR, 2688), bf16), pltpu.VMEM((KR, 2688), f32), dma((8,))],
        compiler_params=pltpu.CompilerParams(vmem_limit_bytes=32 << 20),
        cost_estimate=pl.CostEstimate(flops=1 << 20, bytes_accessed=3 << 20, transcendentals=0),
    )(at_hbm(group_order), at_hbm(head_order), at_hbm(in_weight))
    gated, states, steps = pl.pallas_call(
        kernel,
        out_shape=(
            pltpu.VMEM((ROWS, HPG * HEAD), bf16),
            pltpu.VMEM((ROWS, 2 * N), bf16),
            pltpu.VMEM((HPG, ROWS), f32),
        ),
        in_specs=[anywhere, vmem, vmem, vmem, vmem, vmem],
        out_specs=(vmem, vmem, vmem),
        scratch_shapes=[
            pltpu.VMEM((5, D, CW), bf16),
            pltpu.VMEM((16, 8, KR, 128), bf16),
            pltpu.VMEM((8 * KR, 128), bf16),
            pltpu.VMEM((16 * KR, 128), bf16),
            pltpu.VMEM((HALO + ROWS, D), bf16),
            pltpu.VMEM((HALO + 2 * GRP, CW), f32),
            dma((7,)), dma((7,)), dma((6, 7)), dma((7,)), dma((8,)), dma((7, PIECES)), dma, dma, dma, dma,
        ],
        compiler_params=pltpu.CompilerParams(
            collective_id=0, has_side_effects=True, vmem_limit_bytes=56 << 20
        ),
        cost_estimate=pl.CostEstimate(
            flops=2 * ROWS * D * GW, bytes_accessed=6 << 20, transcendentals=ROWS * GW
        ),
    )(at_hbm(tokens), at_vmem(stage), at_vmem(stage_dt), conv_x, conv_bc, dt_bias.reshape(1, HPG))
    gated, states, steps = pl.pallas_call(
        finish,
        out_shape=(
            pltpu.HBM((ROWS, HPG * HEAD), bf16),
            pltpu.HBM((ROWS, 2 * N), bf16),
            pltpu.HBM((HPG, ROWS), f32),
        ),
        in_specs=[vmem, vmem, vmem],
        out_specs=(anywhere, anywhere, anywhere),
        scratch_shapes=[dma((7,))],
        cost_estimate=pl.CostEstimate(flops=0, bytes_accessed=3 << 20, transcendentals=0),
    )(at_vmem(gated), at_vmem(states), at_vmem(steps))
    return gated, states, steps.T


def solution(mesh):
    return jax.shard_map(
        on_device,
        mesh=mesh,
        in_specs=(
            P(("dp", "tensor"), None),
            P(("dp", "tensor"), None),
            P(),
            P(),
            P(None, "tensor"),
            P(None, "tensor"),
            P("tensor"),
        ),
        out_specs=(P("dp", "tensor"), P("dp", "tensor"), P("dp", "tensor")),
        check_vma=False,
    )
```

```python
import functools

import jax
import jax.numpy as jnp
from jax import lax
from jax.experimental import pallas as pl
from jax.experimental.pallas import tpu as pltpu
from jax.sharding import PartitionSpec as P

MESH = pl.DeviceIdType.MESH
HEAD = 64
HPG = 16
N = 256
GW = 2 * HPG * HEAD + 2 * N + HPG
D = 4096
ROWS = 1024
TOK = 128
PIECES = 4
PIECE = TOK // PIECES
HALF = {"b": slice(0, 256), "c": slice(256, 512)}
KB = 256
KR = 32
GRP = 256
HALO = 16
CW = 512
ORDER = ("dt", 0, 1, 2, 3, "b", "c")
BY_Z = (3, "b")


def arrange(group_order, head_order, weight, stage, stage_dt, held, lined, sems):
    def fetch(slot):
        start = pl.multiple_of(20 * 128 * group_order[slot], 128)
        return pltpu.make_async_copy(weight.at[:, pl.ds(start, 2688)], held.at[slot], sems.at[slot])

    for slot in range(8):
        fetch(slot).start()

    lane = lax.broadcasted_iota(jnp.int32, (KR, 128), 1)
    ten = lax.axis_index("tensor")

    def line_up(slot):
        group = group_order[slot]
        fetch(slot).wait()
        for part in range(4):
            wide = held[slot, :, 640 * part : 640 * part + 768].astype(jnp.float32)
            lined[:, 640 * part : 640 * part + 640] = pltpu.roll(wide, (768 - 16 * group) % 768, 1)[:, :640]
        tile = pltpu.roll(held[slot, :, 2560:2688].astype(jnp.float32), (128 - 16 * group) % 128, 1)
        lined[:, 2560:2688] = jnp.where(lane < HPG, tile, 0.0)

    def head_tile(slot, base, first):
        parts = []
        for half in range(2):
            picked = head_order[slot, first + half]
            start = pl.multiple_of(base + 128 * (picked >> 1), 128)
            tile = lined[:, pl.ds(start, 128)]
            parts.append(jnp.where((picked & 1) == half, tile, pltpu.roll(tile, HEAD, 1)))
        return jnp.where(lane < HEAD, parts[0], parts[1]).astype(jnp.bfloat16)

    def make(chunk, slot, store):
        if chunk == "dt":
            source = jnp.full((128, 128), 128, jnp.int32)
            across = lax.broadcasted_iota(jnp.int32, (128, 128), 1)
            for j in range(HPG):
                source = jnp.where(across == j + HPG * ten, head_order[slot, j], source)
            down = lax.broadcasted_iota(jnp.int32, (128, 128), 0)
            pick = (down == source).astype(jnp.float32).astype(jnp.bfloat16)
            tile = lined[:, 2560:2688].astype(jnp.bfloat16)
            store(0, jnp.dot(tile, pick, preferred_element_type=jnp.float32).astype(jnp.bfloat16))
        elif chunk == 4:
            for tile in range(4):
                store(tile, lined[:, 2048 + 128 * tile : 2176 + 128 * tile].astype(jnp.bfloat16))
        else:
            for part in range(2):
                for pair in range(2):
                    store(2 * part + pair, head_tile(slot, 1024 * part, 4 * chunk + 2 * pair))

    def body(slot, carry):
        line_up(slot)

        def store_dt(tile, value):
            stage_dt[slot] = value

        make("dt", slot, store_dt)
        for chunk in range(5):

            def store(tile, value, chunk=chunk):
                stage[chunk, slot, :, 128 * tile : 128 * tile + 128] = value

            make(chunk, slot, store)
        return carry

    lax.fori_loop(0, 8, body, 0)


def kernel(
    tokens, stage, stage_dt, conv_x, conv_bc, dt_bias,
    gated, states, steps,
    panel, panel_dt, dt_in, dt_all, tok, proj,
    a2a_sem, z_sem, ring_sem, sib_sem, send_sem, t_sem, t_send, h_sem, h_send, own_sem,
):
    dp, ten = lax.axis_index("dp"), lax.axis_index("tensor")
    core, x, zh = dp % 2, (dp // 2) % 4, dp // 8
    y, zl = ten // 2, ten % 2

    def dp_of(zh_, x_, core_):
        return (zh_ * 4 + x_) * 2 + core_

    left, right, opposite = (x + 3) % 4, (x + 1) % 4, (x + 2) % 4
    up, down, far = (y + 1) % 4, (y + 3) % 4, (y + 2) % 4
    at_right = (dp_of(zh, right, core), ten)
    at_left = (dp_of(zh, left, core), ten)
    at_zh = (dp_of(1 - zh, x, core), ten)
    at_sib = (dp_of(zh, x, 1 - core), ten)
    at_up = (dp, up * 2 + zl)
    at_down = (dp, down * 2 + zl)
    at_zl = (dp, y * 2 + 1 - zl)
    after, before = ((dp + 1) % 16, ten), ((dp + 15) % 16, ten)

    load_t = pltpu.make_async_copy(tokens, tok.at[pl.ds(HALO + ten * TOK, TOK)], own_sem)
    load_t.start()

    barrier = pltpu.get_barrier_semaphore()
    for step in range(1, 8):
        pl.semaphore_signal(barrier, inc=1, device_id=(dp, (ten + step) % 8), device_id_type=MESH)
    for peer in (at_right, at_left, at_zh, at_sib, after, before):
        pl.semaphore_signal(barrier, inc=1, device_id=peer, device_id_type=MESH)

    def remote(src, dst, send, recv, peer):
        return pltpu.make_async_remote_copy(
            src_ref=src, dst_ref=dst, send_sem=send, recv_sem=recv, device_id=peer, device_id_type=MESH
        )

    def tok_rows(y_, zl_, piece):
        return tok.at[pl.ds(HALO + (y_ * 2 + zl_) * TOK + piece * PIECE, PIECE)]

    ZL, L0, R0, L1, R1, O0, O1 = range(7)
    arrives = {
        ZL: (y, 1 - zl), L0: (down, zl), R0: (up, zl), L1: (down, 1 - zl),
        R1: (up, 1 - zl), O0: (far, zl), O1: (far, 1 - zl),
    }
    waited = set()

    def tok_wait(*kinds, pieces=range(PIECES)):
        for kind in kinds:
            for piece in pieces:
                if (kind, piece) not in waited:
                    waited.add((kind, piece))
                    ref = tok_rows(*arrives[kind], piece)
                    pltpu.make_async_copy(ref, ref, t_sem.at[kind, piece]).wait()

    def tok_send(ref, dst, kind, piece, peer):
        remote(ref, dst, t_send, t_sem.at[kind, piece], peer).start()

    def slot(q):
        piece = PIECES - 1 - q % PIECES
        if q < PIECES:
            src, dst = tokens.at[pl.ds(piece * PIECE, PIECE)], tok_rows(y, zl, piece)
            tok_send(src, dst, L0, piece, at_up)
            tok_send(src, dst, R0, piece, at_down)
        elif q < 2 * PIECES:
            tok_wait(ZL, pieces=(piece,))
            ref = tok_rows(y, 1 - zl, piece)
            tok_send(ref, ref, L1, piece, at_up)
            tok_send(ref, ref, R1, piece, at_down)
        else:
            tok_wait(L0, R1, pieces=(piece,))
            ref = tok_rows(down, zl, piece)
            tok_send(ref, ref, O0, piece, at_up)
            ref = tok_rows(up, 1 - zl, piece)
            tok_send(ref, ref, O1, piece, at_down)

    def across(piece):
        src, dst = tokens.at[pl.ds(piece * PIECE, PIECE)], tok_rows(y, zl, piece)
        tok_send(src, dst, ZL, piece, at_zl)

    def tok_near():
        tok_wait(ZL, L0, R0, L1, R1)

    def tok_far():
        tok_wait(O0, O1)

    head = tok.at[pl.ds(0, HALO)]

    def halo_send(where, src, *peers):
        @pl.when(where)
        def _():
            for peer in peers:
                remote(src, head, h_send, h_sem, peer).start()

    def halo_wait(where):
        @pl.when(jnp.logical_and(where, dp > 0))
        def _():
            pltpu.make_async_copy(head, head, h_sem).wait()

    def halo_sent(where, count):
        @pl.when(where)
        def _():
            for _ in range(count):
                pltpu.make_async_copy(head, head, h_send).wait()

    halo_first = jnp.logical_and(ten == 7, dp < 15)
    halo_a = ten == 7
    halo_b = ten == 6
    halo_c = ten == 1
    halo_d = ten == 4
    halo_e = ten == 0
    halo_rest = jnp.logical_or(ten == 5, y == 1)
    inner = dp > 0

    @pl.when(dp == 0)
    def _():
        tok[0:HALO, :] = jnp.zeros((HALO, D), jnp.bfloat16)

    def rows_of(chunk, start, size):
        if chunk == "dt":
            return dt_all.at[pl.ds(start, size)]
        if chunk in ("b", "c"):
            return panel.at[4, pl.ds(start, size), HALF[chunk]]
        return panel.at[chunk, pl.ds(start, size)]

    def sem_of(chunk):
        return ORDER.index(chunk)

    def height(chunk):
        return KR if chunk == "dt" else KB

    def block(chunk, zh_, x_, core_):
        return rows_of(chunk, dp_of(zh_, x_, core_) * height(chunk), height(chunk))

    def prepare(chunk):
        if chunk == "dt":
            dst, sent = dt_in.at[pl.ds(ten * KR, KR)], send_sem.at[len(ORDER)]
        else:
            dst, sent = rows_of(chunk, dp * KB + ten * KR, KR), send_sem.at[sem_of(chunk)]
        sem = a2a_sem.at[sem_of(chunk)]

        def source(slot):
            if chunk == "dt":
                return stage_dt.at[slot]
            if chunk in ("b", "c"):
                return stage.at[4, slot, :, HALF[chunk]]
            return stage.at[chunk, slot]

        for step in range(1, 8):
            slot = (ten + step) % 8
            remote(source(slot), dst, sent, sem, (dp, slot)).start()
        pltpu.make_async_copy(source(ten), dst, sem).start()

    def send(chunk, ref, recv, peer):
        remote(ref, ref, send_sem.at[sem_of(chunk)], recv.at[sem_of(chunk)], peer).start()

    def wait(chunk, ref, sem):
        pltpu.make_async_copy(ref, ref, sem.at[sem_of(chunk)]).wait()

    def ring(kind):
        return ring_sem.at[kind]

    RL0, RR0, RL1, RR1, RO0, RO1 = range(6)

    def s_z(chunk):
        send(chunk, block(chunk, zh, x, core), z_sem, at_zh)

    def s_ready(chunk):
        if chunk == "dt":
            pltpu.make_async_copy(dt_in, dt_in, a2a_sem.at[sem_of(chunk)]).wait()
            total = dt_in[0:KR, :].astype(jnp.float32)
            for sender in range(1, 8):
                total = total + dt_in[KR * sender : KR * sender + KR, :].astype(jnp.float32)
            dt_all[pl.ds(dp * KR, KR), :] = total.astype(jnp.bfloat16)
        else:
            wait(chunk, block(chunk, zh, x, core), a2a_sem)

    def s_own(chunk):
        ref = block(chunk, zh, x, core)
        send(chunk, ref, ring(RL0), at_right)
        send(chunk, ref, ring(RR0), at_left)
        send(chunk, ref, sib_sem, at_sib)

    def s_pair(chunk):
        ref = block(chunk, 1 - zh, x, core)
        wait(chunk, ref, z_sem)
        if chunk not in BY_Z:
            send(chunk, ref, ring(RL1), at_right)
            send(chunk, ref, ring(RR1), at_left)
        send(chunk, ref, sib_sem, at_sib)

    def s_right(chunk):
        ref = block(chunk, zh, right, core)
        wait(chunk, ref, ring(RR0))
        if chunk in BY_Z:
            send(chunk, ref, ring(RR1), at_zh)
        send(chunk, ref, sib_sem, at_sib)

    def s_near(chunk):
        ref = block(chunk, zh, left, core)
        wait(chunk, ref, ring(RL0))
        send(chunk, ref, ring(RO0), at_right)
        if chunk in BY_Z:
            send(chunk, ref, ring(RL1), at_zh)
        send(chunk, ref, sib_sem, at_sib)
        if chunk in BY_Z:
            s_right(chunk)

    def s_next(chunk):
        ref = block(chunk, 1 - zh, right, core)
        wait(chunk, ref, ring(RR1))
        send(chunk, ref, ring(RO1), at_left)
        send(chunk, ref, sib_sem, at_sib)

    def s_far(chunk):
        if chunk not in BY_Z:
            s_right(chunk)
        ref = block(chunk, 1 - zh, left, core)
        wait(chunk, ref, ring(RL1))
        send(chunk, ref, sib_sem, at_sib)
        ref = block(chunk, zh, opposite, core)
        wait(chunk, ref, ring(RO0))
        send(chunk, ref, sib_sem, at_sib)
        ref = block(chunk, 1 - zh, opposite, core)
        wait(chunk, ref, ring(RO1))
        send(chunk, ref, sib_sem, at_sib)

    def s_sib(chunk):
        wait(chunk, rows_of(chunk, 0, 8 * height(chunk)), sib_sem)

    def unpack():
        packed = dt_all[...].astype(jnp.float32)
        for sender in range(8):
            turned = pltpu.roll(packed, (128 - HPG * sender) % 128, 1)
            panel_dt[:, sender] = turned.reshape(16, KR, 128).astype(jnp.bfloat16)

    def silu(v):
        return 0.5 * v * (1.0 + jnp.tanh(0.5 * v))

    def rounded(v):
        return v.astype(jnp.bfloat16).astype(jnp.float32)

    def conv(taps, size, col):
        total = taps[0:1, :] * proj[pl.ds(HALO - 3, size), col : col + 256]
        for k in range(1, 4):
            total = total + taps[k : k + 1, :] * proj[pl.ds(HALO - 3 + k, size), col : col + 256]
        return total

    def unit(start, size, chunk):
        lhs = tok[pl.ds(start, HALO + size), :]
        into = pl.ds(0, HALO + size)
        if chunk in ("b", "c"):
            cols = HALF[chunk]
            spot = HALF["b" if (start // size) % 2 else "c"]
            proj[into, spot] = rounded(jnp.dot(lhs, panel[4, :, cols], preferred_element_type=jnp.float32))
            states[pl.ds(start, size), cols] = silu(conv(conv_bc[:, cols], size, spot.start)).astype(jnp.bfloat16)
        else:
            for half in HALF.values():
                proj[into, half] = rounded(jnp.dot(lhs, panel[chunk, :, half], preferred_element_type=jnp.float32))
            cols = slice(256 * chunk, 256 * chunk + 256)
            value = silu(conv(conv_x[:, cols], size, 256)) * silu(proj[pl.ds(HALO, size), 0:256])
            gated[pl.ds(start, size), cols] = value.astype(jnp.bfloat16)

    def whole(chunk):
        for step in range(2):
            unit(step * 2 * GRP, 2 * GRP, chunk)

    def unit_dt(group):
        start = pl.multiple_of(group * GRP, GRP)
        raw = rounded(jnp.dot(tok[pl.ds(start + HALO, GRP), :], panel_dt[...].reshape(D, 128), preferred_element_type=jnp.float32))
        value = (raw[:, :HPG] + dt_bias[...]).T
        steps[:, pl.ds(start, GRP)] = jnp.maximum(value, 0.0) + jnp.log1p(jnp.exp(-jnp.abs(value)))

    def units(places, *chunks):
        for place in places:
            for chunk in chunks:
                if chunk == "dt":
                    unit_dt(groups[place])
                else:
                    unit(pl.multiple_of(groups[place] * GRP, GRP), GRP, chunk)

    groups = (y, up, down, far)

    pl.semaphore_wait(barrier, 13)
    prepare(0)
    halo_send(halo_first, tokens.at[pl.ds(TOK - HALO, HALO)], after)
    prepare(1)
    prepare("dt")
    s_ready(0)
    s_z(0)
    s_own(0)
    prepare(2)
    slot(0)
    s_ready(1)
    s_own(1)
    s_near(0)
    across(3)
    slot(1)
    halo_wait(halo_a)
    halo_send(jnp.logical_and(halo_a, inner), head, at_zl, at_up, at_down)
    s_pair(0)
    s_z(1)
    s_ready("dt")
    s_z("dt")
    s_own("dt")
    prepare(3)
    slot(2)
    across(2)
    s_next(0)
    s_near(1)
    across(1)
    s_pair(1)
    s_ready(2)
    s_own(2)
    s_z(2)
    slot(3)
    halo_wait(halo_b)
    halo_send(jnp.logical_and(halo_b, inner), head, at_up, at_down)
    slot(4)
    prepare("b")
    s_near("dt")
    s_pair("dt")
    across(0)
    slot(5)
    s_next(1)
    s_near(2)
    slot(6)
    prepare("c")
    s_pair(2)
    s_ready(3)
    s_own(3)
    s_z(3)
    slot(7)
    s_next("dt")
    s_far(0)
    halo_wait(jnp.logical_or(halo_c, halo_d))
    halo_send(jnp.logical_and(halo_c, inner), head, at_up)
    halo_send(jnp.logical_and(halo_d, inner), head, at_down)
    slot(8)
    s_next(2)
    s_ready("b")
    s_own("b")
    load_t.wait()
    halo_wait(halo_e)
    tok_wait(ZL)
    tok_wait(L0, L1, pieces=(3,))
    s_sib(0)
    units((0,), 0)
    s_near(3)
    s_z("b")
    s_far(1)
    s_pair(3)
    slot(9)
    tok_wait(L0, R0, L1, R1)
    units((1,), 0)
    s_ready("c")
    s_own("c")
    s_z("c")
    s_far("dt")
    s_near("b")
    slot(10)
    s_sib(1)
    units((0, 1), 1)
    s_far(2)
    slot(11)
    tok_wait(O0, O1, pieces=(3,))
    halo_wait(halo_rest)
    units((2,), 0, 1)
    s_next(3)
    s_pair("b")
    s_near("c")
    s_sib("dt")
    unpack()
    units((0, 1, 2), "dt")
    s_pair("c")
    s_sib(2)
    units((0, 1), 2)
    s_next("b")
    tok_far()
    units((3,), "dt", 0)
    s_next("c")
    s_far(3)
    units((2,), 2)
    units((3,), 1, 2)
    s_far("b")
    s_far("c")
    s_sib(3)
    units((0, 1, 2, 3), 3)
    s_sib("b")
    s_sib("c")
    whole("b")
    whole("c")

    pltpu.make_async_copy(tok.at[pl.ds(0, 7 * TOK)], tok.at[pl.ds(0, 7 * TOK)], t_send).wait()

    halo_sent(halo_first, 1)
    halo_sent(jnp.logical_and(halo_a, inner), 3)
    halo_sent(jnp.logical_and(halo_b, inner), 2)
    halo_sent(jnp.logical_and(jnp.logical_or(halo_c, halo_d), inner), 1)

    for chunk in ORDER[1:]:
        wait(chunk, rows_of(chunk, 0, 15 * KB + 7 * KR), send_sem)
    wait("dt", rows_of("dt", 0, 15 * KR), send_sem)
    ref = dt_in.at[pl.ds(0, 7 * KR)]
    pltpu.make_async_copy(ref, ref, send_sem.at[len(ORDER)]).wait()


def finish(gated_v, states_v, steps_v, gated, states, steps, sems):
    copies = [pltpu.make_async_copy(steps_v, steps, sems.at[6])]
    for part in range(4):
        rows = pl.ds(GRP * part, GRP)
        copies.append(pltpu.make_async_copy(gated_v.at[rows], gated.at[rows], sems.at[part]))
    for part in range(2):
        rows = pl.ds(2 * GRP * part, 2 * GRP)
        copies.append(pltpu.make_async_copy(states_v.at[rows], states.at[rows], sems.at[4 + part]))
    for copy in copies:
        copy.start()
    for copy in copies:
        copy.wait()


def on_device(tokens, in_weight, group_order, head_order, conv_x, conv_bc, dt_bias):
    vmem, smem, anywhere = (
        pl.BlockSpec(memory_space=pltpu.VMEM),
        pl.BlockSpec(memory_space=pltpu.SMEM),
        pl.BlockSpec(memory_space=pl.ANY),
    )
    dma = pltpu.SemaphoreType.DMA
    bf16, f32 = jnp.bfloat16, jnp.float32
    def at_vmem(value):
        return pltpu.with_memory_space_constraint(value, pltpu.VMEM)

    def at_hbm(value):
        return pltpu.with_memory_space_constraint(value, pltpu.HBM)

    stage, stage_dt = pl.pallas_call(
        arrange,
        out_shape=(pltpu.VMEM((5, 8, KR, CW), bf16), pltpu.VMEM((8, KR, 128), bf16)),
        in_specs=[smem, smem, anywhere],
        out_specs=(vmem, vmem),
        scratch_shapes=[pltpu.VMEM((8, KR, 2688), bf16), pltpu.VMEM((KR, 2688), f32), dma((8,))],
        compiler_params=pltpu.CompilerParams(vmem_limit_bytes=32 << 20),
        cost_estimate=pl.CostEstimate(flops=1 << 20, bytes_accessed=3 << 20, transcendentals=0),
    )(at_hbm(group_order), at_hbm(head_order), at_hbm(in_weight))
    gated, states, steps = pl.pallas_call(
        kernel,
        out_shape=(
            pltpu.VMEM((ROWS, HPG * HEAD), bf16),
            pltpu.VMEM((ROWS, 2 * N), bf16),
            pltpu.VMEM((HPG, ROWS), f32),
        ),
        in_specs=[anywhere, vmem, vmem, vmem, vmem, vmem],
        out_specs=(vmem, vmem, vmem),
        scratch_shapes=[
            pltpu.VMEM((5, D, CW), bf16),
            pltpu.VMEM((16, 8, KR, 128), bf16),
            pltpu.VMEM((8 * KR, 128), bf16),
            pltpu.VMEM((16 * KR, 128), bf16),
            pltpu.VMEM((HALO + ROWS, D), bf16),
            pltpu.VMEM((HALO + 2 * GRP, CW), f32),
            dma((7,)), dma((7,)), dma((6, 7)), dma((7,)), dma((8,)), dma((7, PIECES)), dma, dma, dma, dma,
        ],
        compiler_params=pltpu.CompilerParams(
            collective_id=0, has_side_effects=True, vmem_limit_bytes=56 << 20
        ),
        cost_estimate=pl.CostEstimate(
            flops=2 * ROWS * D * GW, bytes_accessed=6 << 20, transcendentals=ROWS * GW
        ),
    )(at_hbm(tokens), at_vmem(stage), at_vmem(stage_dt), conv_x, conv_bc, dt_bias.reshape(1, HPG))
    gated, states, steps = pl.pallas_call(
        finish,
        out_shape=(
            pltpu.HBM((ROWS, HPG * HEAD), bf16),
            pltpu.HBM((ROWS, 2 * N), bf16),
            pltpu.HBM((HPG, ROWS), f32),
        ),
        in_specs=[vmem, vmem, vmem],
        out_specs=(anywhere, anywhere, anywhere),
        scratch_shapes=[dma((7,))],
        cost_estimate=pl.CostEstimate(flops=0, bytes_accessed=3 << 20, transcendentals=0),
    )(at_vmem(gated), at_vmem(states), at_vmem(steps))
    return gated, states, steps.T


def solution(mesh):
    return jax.shard_map(
        on_device,
        mesh=mesh,
        in_specs=(
            P(("dp", "tensor"), None),
            P(("dp", "tensor"), None),
            P(),
            P(),
            P(None, "tensor"),
            P(None, "tensor"),
            P("tensor"),
        ),
        out_specs=(P("dp", "tensor"), P("dp", "tensor"), P("dp", "tensor")),
        check_vma=False,
    )
```

```python
import functools

import jax
import jax.numpy as jnp
from jax import lax
from jax.experimental import pallas as pl
from jax.experimental.pallas import tpu as pltpu
from jax.sharding import PartitionSpec as P

MESH = pl.DeviceIdType.MESH
HEAD = 64
HPG = 16
N = 256
GW = 2 * HPG * HEAD + 2 * N + HPG
D = 4096
ROWS = 1024
TOK = 128
PIECES = 4
PIECE = TOK // PIECES
HALF = {"b": slice(0, 256), "c": slice(256, 512)}
KB = 256
KR = 32
GRP = 256
HALO = 16
CW = 512
ORDER = ("dt", 0, 1, 2, 3, "b", "c")
BY_Z = ("b",)


def arrange(group_order, head_order, weight, stage, stage_dt, held, lined, sems):
    def fetch(slot):
        start = pl.multiple_of(20 * 128 * group_order[slot], 128)
        return pltpu.make_async_copy(weight.at[:, pl.ds(start, 2688)], held.at[slot], sems.at[slot])

    for slot in range(8):
        fetch(slot).start()

    lane = lax.broadcasted_iota(jnp.int32, (KR, 128), 1)
    ten = lax.axis_index("tensor")

    def line_up(slot):
        group = group_order[slot]
        fetch(slot).wait()
        for part in range(4):
            wide = held[slot, :, 640 * part : 640 * part + 768].astype(jnp.float32)
            lined[:, 640 * part : 640 * part + 640] = pltpu.roll(wide, (768 - 16 * group) % 768, 1)[:, :640]
        tile = pltpu.roll(held[slot, :, 2560:2688].astype(jnp.float32), (128 - 16 * group) % 128, 1)
        lined[:, 2560:2688] = jnp.where(lane < HPG, tile, 0.0)

    def head_tile(slot, base, first):
        parts = []
        for half in range(2):
            picked = head_order[slot, first + half]
            start = pl.multiple_of(base + 128 * (picked >> 1), 128)
            tile = lined[:, pl.ds(start, 128)]
            parts.append(jnp.where((picked & 1) == half, tile, pltpu.roll(tile, HEAD, 1)))
        return jnp.where(lane < HEAD, parts[0], parts[1]).astype(jnp.bfloat16)

    def make(chunk, slot, store):
        if chunk == "dt":
            source = jnp.full((128, 128), 128, jnp.int32)
            across = lax.broadcasted_iota(jnp.int32, (128, 128), 1)
            for j in range(HPG):
                source = jnp.where(across == j + HPG * ten, head_order[slot, j], source)
            down = lax.broadcasted_iota(jnp.int32, (128, 128), 0)
            pick = (down == source).astype(jnp.float32).astype(jnp.bfloat16)
            tile = lined[:, 2560:2688].astype(jnp.bfloat16)
            store(0, jnp.dot(tile, pick, preferred_element_type=jnp.float32).astype(jnp.bfloat16))
        elif chunk == 4:
            for tile in range(4):
                store(tile, lined[:, 2048 + 128 * tile : 2176 + 128 * tile].astype(jnp.bfloat16))
        else:
            for part in range(2):
                for pair in range(2):
                    store(2 * part + pair, head_tile(slot, 1024 * part, 4 * chunk + 2 * pair))

    def body(slot, carry):
        line_up(slot)

        def store_dt(tile, value):
            stage_dt[slot] = value

        make("dt", slot, store_dt)
        for chunk in range(5):

            def store(tile, value, chunk=chunk):
                stage[chunk, slot, :, 128 * tile : 128 * tile + 128] = value

            make(chunk, slot, store)
        return carry

    lax.fori_loop(0, 8, body, 0)


def kernel(
    tokens, stage, stage_dt, conv_x, conv_bc, dt_bias,
    gated, states, steps,
    panel, panel_dt, dt_in, dt_all, tok, proj,
    a2a_sem, z_sem, ring_sem, sib_sem, send_sem, t_sem, t_send, h_sem, h_send, own_sem,
):
    dp, ten = lax.axis_index("dp"), lax.axis_index("tensor")
    core, x, zh = dp % 2, (dp // 2) % 4, dp // 8
    y, zl = ten // 2, ten % 2

    def dp_of(zh_, x_, core_):
        return (zh_ * 4 + x_) * 2 + core_

    left, right, opposite = (x + 3) % 4, (x + 1) % 4, (x + 2) % 4
    up, down, far = (y + 1) % 4, (y + 3) % 4, (y + 2) % 4
    at_right = (dp_of(zh, right, core), ten)
    at_left = (dp_of(zh, left, core), ten)
    at_zh = (dp_of(1 - zh, x, core), ten)
    at_sib = (dp_of(zh, x, 1 - core), ten)
    at_up = (dp, up * 2 + zl)
    at_down = (dp, down * 2 + zl)
    at_zl = (dp, y * 2 + 1 - zl)
    after, before = ((dp + 1) % 16, ten), ((dp + 15) % 16, ten)

    load_t = pltpu.make_async_copy(tokens, tok.at[pl.ds(HALO + ten * TOK, TOK)], own_sem)
    load_t.start()

    barrier = pltpu.get_barrier_semaphore()
    for step in range(1, 8):
        pl.semaphore_signal(barrier, inc=1, device_id=(dp, (ten + step) % 8), device_id_type=MESH)
    for peer in (at_right, at_left, at_zh, at_sib, after, before):
        pl.semaphore_signal(barrier, inc=1, device_id=peer, device_id_type=MESH)

    def remote(src, dst, send, recv, peer):
        return pltpu.make_async_remote_copy(
            src_ref=src, dst_ref=dst, send_sem=send, recv_sem=recv, device_id=peer, device_id_type=MESH
        )

    def tok_rows(y_, zl_, piece):
        return tok.at[pl.ds(HALO + (y_ * 2 + zl_) * TOK + piece * PIECE, PIECE)]

    ZL, L0, R0, L1, R1, O0, O1 = range(7)
    arrives = {
        ZL: (y, 1 - zl), L0: (down, zl), R0: (up, zl), L1: (down, 1 - zl),
        R1: (up, 1 - zl), O0: (far, zl), O1: (far, 1 - zl),
    }
    waited = set()

    def tok_wait(*kinds, pieces=range(PIECES)):
        for kind in kinds:
            for piece in pieces:
                if (kind, piece) not in waited:
                    waited.add((kind, piece))
                    ref = tok_rows(*arrives[kind], piece)
                    pltpu.make_async_copy(ref, ref, t_sem.at[kind, piece]).wait()

    def tok_send(ref, dst, kind, piece, peer):
        remote(ref, dst, t_send, t_sem.at[kind, piece], peer).start()

    def slot(q):
        piece = PIECES - 1 - q % PIECES
        if q < PIECES:
            src, dst = tokens.at[pl.ds(piece * PIECE, PIECE)], tok_rows(y, zl, piece)
            tok_send(src, dst, L0, piece, at_up)
            tok_send(src, dst, R0, piece, at_down)
        elif q < 2 * PIECES:
            tok_wait(ZL, pieces=(piece,))
            ref = tok_rows(y, 1 - zl, piece)
            tok_send(ref, ref, L1, piece, at_up)
            tok_send(ref, ref, R1, piece, at_down)
        else:
            tok_wait(L0, R1, pieces=(piece,))
            ref = tok_rows(down, zl, piece)
            tok_send(ref, ref, O0, piece, at_up)
            ref = tok_rows(up, 1 - zl, piece)
            tok_send(ref, ref, O1, piece, at_down)

    def across(piece):
        src, dst = tokens.at[pl.ds(piece * PIECE, PIECE)], tok_rows(y, zl, piece)
        tok_send(src, dst, ZL, piece, at_zl)

    def tok_near():
        tok_wait(ZL, L0, R0, L1, R1)

    def tok_far():
        tok_wait(O0, O1)

    head = tok.at[pl.ds(0, HALO)]

    def halo_send(where, src, *peers):
        @pl.when(where)
        def _():
            for peer in peers:
                remote(src, head, h_send, h_sem, peer).start()

    def halo_wait(where):
        @pl.when(jnp.logical_and(where, dp > 0))
        def _():
            pltpu.make_async_copy(head, head, h_sem).wait()

    def halo_sent(where, count):
        @pl.when(where)
        def _():
            for _ in range(count):
                pltpu.make_async_copy(head, head, h_send).wait()

    halo_first = jnp.logical_and(ten == 7, dp < 15)
    halo_a = ten == 7
    halo_b = ten == 6
    halo_c = ten == 1
    halo_d = ten == 4
    halo_e = ten == 0
    halo_rest = jnp.logical_or(ten == 5, y == 1)
    inner = dp > 0

    @pl.when(dp == 0)
    def _():
        tok[0:HALO, :] = jnp.zeros((HALO, D), jnp.bfloat16)

    def rows_of(chunk, start, size):
        if chunk == "dt":
            return dt_all.at[pl.ds(start, size)]
        if chunk in ("b", "c"):
            return panel.at[4, pl.ds(start, size), HALF[chunk]]
        return panel.at[chunk, pl.ds(start, size)]

    def sem_of(chunk):
        return ORDER.index(chunk)

    def height(chunk):
        return KR if chunk == "dt" else KB

    def block(chunk, zh_, x_, core_):
        return rows_of(chunk, dp_of(zh_, x_, core_) * height(chunk), height(chunk))

    def prepare(chunk):
        if chunk == "dt":
            dst, sent = dt_in.at[pl.ds(ten * KR, KR)], send_sem.at[len(ORDER)]
        else:
            dst, sent = rows_of(chunk, dp * KB + ten * KR, KR), send_sem.at[sem_of(chunk)]
        sem = a2a_sem.at[sem_of(chunk)]

        def source(slot):
            if chunk == "dt":
                return stage_dt.at[slot]
            if chunk in ("b", "c"):
                return stage.at[4, slot, :, HALF[chunk]]
            return stage.at[chunk, slot]

        for step in range(1, 8):
            slot = (ten + step) % 8
            remote(source(slot), dst, sent, sem, (dp, slot)).start()
        pltpu.make_async_copy(source(ten), dst, sem).start()

    def send(chunk, ref, recv, peer):
        remote(ref, ref, send_sem.at[sem_of(chunk)], recv.at[sem_of(chunk)], peer).start()

    def wait(chunk, ref, sem):
        pltpu.make_async_copy(ref, ref, sem.at[sem_of(chunk)]).wait()

    def ring(kind):
        return ring_sem.at[kind]

    RL0, RR0, RL1, RR1, RO0, RO1 = range(6)

    def s_z(chunk):
        send(chunk, block(chunk, zh, x, core), z_sem, at_zh)

    def s_ready(chunk):
        if chunk == "dt":
            pltpu.make_async_copy(dt_in, dt_in, a2a_sem.at[sem_of(chunk)]).wait()
            total = dt_in[0:KR, :].astype(jnp.float32)
            for sender in range(1, 8):
                total = total + dt_in[KR * sender : KR * sender + KR, :].astype(jnp.float32)
            dt_all[pl.ds(dp * KR, KR), :] = total.astype(jnp.bfloat16)
        else:
            wait(chunk, block(chunk, zh, x, core), a2a_sem)

    def s_own(chunk):
        ref = block(chunk, zh, x, core)
        send(chunk, ref, ring(RL0), at_right)
        send(chunk, ref, ring(RR0), at_left)
        send(chunk, ref, sib_sem, at_sib)

    def s_pair(chunk):
        ref = block(chunk, 1 - zh, x, core)
        wait(chunk, ref, z_sem)
        if chunk not in BY_Z:
            send(chunk, ref, ring(RL1), at_right)
            send(chunk, ref, ring(RR1), at_left)
        send(chunk, ref, sib_sem, at_sib)

    def s_right(chunk):
        ref = block(chunk, zh, right, core)
        wait(chunk, ref, ring(RR0))
        if chunk in BY_Z:
            send(chunk, ref, ring(RR1), at_zh)
        send(chunk, ref, sib_sem, at_sib)

    def s_near(chunk):
        ref = block(chunk, zh, left, core)
        wait(chunk, ref, ring(RL0))
        send(chunk, ref, ring(RO0), at_right)
        if chunk in BY_Z:
            send(chunk, ref, ring(RL1), at_zh)
        send(chunk, ref, sib_sem, at_sib)
        if chunk in BY_Z:
            s_right(chunk)

    def s_next(chunk):
        ref = block(chunk, 1 - zh, right, core)
        wait(chunk, ref, ring(RR1))
        send(chunk, ref, ring(RO1), at_left)
        send(chunk, ref, sib_sem, at_sib)

    def s_far(chunk):
        if chunk not in BY_Z:
            s_right(chunk)
        ref = block(chunk, 1 - zh, left, core)
        wait(chunk, ref, ring(RL1))
        send(chunk, ref, sib_sem, at_sib)
        ref = block(chunk, zh, opposite, core)
        wait(chunk, ref, ring(RO0))
        send(chunk, ref, sib_sem, at_sib)
        ref = block(chunk, 1 - zh, opposite, core)
        wait(chunk, ref, ring(RO1))
        send(chunk, ref, sib_sem, at_sib)

    def s_sib(chunk):
        wait(chunk, rows_of(chunk, 0, 8 * height(chunk)), sib_sem)

    def unpack():
        packed = dt_all[...].astype(jnp.float32)
        for sender in range(8):
            turned = pltpu.roll(packed, (128 - HPG * sender) % 128, 1)
            panel_dt[:, sender] = turned.reshape(16, KR, 128).astype(jnp.bfloat16)

    def silu(v):
        return 0.5 * v * (1.0 + jnp.tanh(0.5 * v))

    def rounded(v):
        return v.astype(jnp.bfloat16).astype(jnp.float32)

    def conv(taps, size, col):
        total = taps[0:1, :] * proj[pl.ds(HALO - 3, size), col : col + 256]
        for k in range(1, 4):
            total = total + taps[k : k + 1, :] * proj[pl.ds(HALO - 3 + k, size), col : col + 256]
        return total

    def unit(start, size, chunk):
        lhs = tok[pl.ds(start, HALO + size), :]
        into = pl.ds(0, HALO + size)
        if chunk in ("b", "c"):
            cols = HALF[chunk]
            spot = HALF["b" if (start // size) % 2 else "c"]
            proj[into, spot] = rounded(jnp.dot(lhs, panel[4, :, cols], preferred_element_type=jnp.float32))
            states[pl.ds(start, size), cols] = silu(conv(conv_bc[:, cols], size, spot.start)).astype(jnp.bfloat16)
        else:
            for half in HALF.values():
                proj[into, half] = rounded(jnp.dot(lhs, panel[chunk, :, half], preferred_element_type=jnp.float32))
            cols = slice(256 * chunk, 256 * chunk + 256)
            value = silu(conv(conv_x[:, cols], size, 256)) * silu(proj[pl.ds(HALO, size), 0:256])
            gated[pl.ds(start, size), cols] = value.astype(jnp.bfloat16)

    def whole(chunk):
        for step in range(2):
            unit(step * 2 * GRP, 2 * GRP, chunk)

    def unit_dt(group):
        start = pl.multiple_of(group * GRP, GRP)
        raw = rounded(jnp.dot(tok[pl.ds(start + HALO, GRP), :], panel_dt[...].reshape(D, 128), preferred_element_type=jnp.float32))
        value = (raw[:, :HPG] + dt_bias[...]).T
        steps[:, pl.ds(start, GRP)] = jnp.maximum(value, 0.0) + jnp.log1p(jnp.exp(-jnp.abs(value)))

    def units(places, *chunks):
        for place in places:
            for chunk in chunks:
                if chunk == "dt":
                    unit_dt(groups[place])
                else:
                    unit(pl.multiple_of(groups[place] * GRP, GRP), GRP, chunk)

    groups = (y, up, down, far)

    pl.semaphore_wait(barrier, 13)
    prepare(0)
    halo_send(halo_first, tokens.at[pl.ds(TOK - HALO, HALO)], after)
    prepare(1)
    prepare("dt")
    s_ready(0)
    s_z(0)
    s_own(0)
    prepare(2)
    slot(0)
    s_ready(1)
    s_own(1)
    s_near(0)
    across(3)
    slot(1)
    halo_wait(halo_a)
    halo_send(jnp.logical_and(halo_a, inner), head, at_zl, at_up, at_down)
    s_pair(0)
    s_z(1)
    s_ready("dt")
    s_z("dt")
    s_own("dt")
    prepare(3)
    slot(2)
    across(2)
    s_next(0)
    s_near(1)
    across(1)
    s_pair(1)
    s_ready(2)
    s_own(2)
    s_z(2)
    slot(3)
    halo_wait(halo_b)
    halo_send(jnp.logical_and(halo_b, inner), head, at_up, at_down)
    slot(4)
    prepare("b")
    s_near("dt")
    s_pair("dt")
    across(0)
    slot(5)
    s_next(1)
    s_near(2)
    slot(6)
    prepare("c")
    s_pair(2)
    s_ready(3)
    s_own(3)
    s_z(3)
    slot(7)
    s_next("dt")
    s_far(0)
    halo_wait(jnp.logical_or(halo_c, halo_d))
    halo_send(jnp.logical_and(halo_c, inner), head, at_up)
    halo_send(jnp.logical_and(halo_d, inner), head, at_down)
    slot(8)
    s_next(2)
    s_ready("b")
    s_own("b")
    load_t.wait()
    halo_wait(halo_e)
    tok_wait(ZL)
    tok_wait(L0, L1, pieces=(3,))
    s_sib(0)
    units((0,), 0)
    s_near(3)
    s_z("b")
    s_far(1)
    s_pair(3)
    slot(9)
    tok_wait(L0, R0, L1, R1)
    units((1,), 0)
    s_ready("c")
    s_own("c")
    s_z("c")
    s_far("dt")
    slot(10)
    s_sib(1)
    units((0, 1), 1)
    s_near("b")
    s_far(2)
    slot(11)
    tok_wait(O0, O1, pieces=(3,))
    halo_wait(halo_rest)
    units((2,), 0, 1)
    s_next(3)
    s_sib("dt")
    unpack()
    units((0, 1, 2), "dt")
    s_sib(2)
    units((0, 1, 2), 2)
    s_near("c")
    s_pair("b")
    s_pair("c")
    s_far(3)
    s_next("b")
    tok_far()
    units((3,), "dt", 0, 1)
    s_next("c")
    s_sib(3)
    units((3,), 2)
    units((0, 1), 3)
    s_far("b")
    s_far("c")
    units((2, 3), 3)
    s_sib("b")
    whole("b")
    s_sib("c")
    whole("c")

    pltpu.make_async_copy(tok.at[pl.ds(0, 7 * TOK)], tok.at[pl.ds(0, 7 * TOK)], t_send).wait()

    halo_sent(halo_first, 1)
    halo_sent(jnp.logical_and(halo_a, inner), 3)
    halo_sent(jnp.logical_and(halo_b, inner), 2)
    halo_sent(jnp.logical_and(jnp.logical_or(halo_c, halo_d), inner), 1)

    for chunk in ORDER[1:]:
        wait(chunk, rows_of(chunk, 0, 15 * KB + 7 * KR), send_sem)
    wait("dt", rows_of("dt", 0, 15 * KR), send_sem)
    ref = dt_in.at[pl.ds(0, 7 * KR)]
    pltpu.make_async_copy(ref, ref, send_sem.at[len(ORDER)]).wait()


def finish(gated_v, states_v, steps_v, gated, states, steps, sems):
    copies = [pltpu.make_async_copy(steps_v, steps, sems.at[6])]
    for part in range(4):
        rows = pl.ds(GRP * part, GRP)
        copies.append(pltpu.make_async_copy(gated_v.at[rows], gated.at[rows], sems.at[part]))
    for part in range(2):
        rows = pl.ds(2 * GRP * part, 2 * GRP)
        copies.append(pltpu.make_async_copy(states_v.at[rows], states.at[rows], sems.at[4 + part]))
    for copy in copies:
        copy.start()
    for copy in copies:
        copy.wait()


def on_device(tokens, in_weight, group_order, head_order, conv_x, conv_bc, dt_bias):
    vmem, smem, anywhere = (
        pl.BlockSpec(memory_space=pltpu.VMEM),
        pl.BlockSpec(memory_space=pltpu.SMEM),
        pl.BlockSpec(memory_space=pl.ANY),
    )
    dma = pltpu.SemaphoreType.DMA
    bf16, f32 = jnp.bfloat16, jnp.float32
    def at_vmem(value):
        return pltpu.with_memory_space_constraint(value, pltpu.VMEM)

    def at_hbm(value):
        return pltpu.with_memory_space_constraint(value, pltpu.HBM)

    stage, stage_dt = pl.pallas_call(
        arrange,
        out_shape=(pltpu.VMEM((5, 8, KR, CW), bf16), pltpu.VMEM((8, KR, 128), bf16)),
        in_specs=[smem, smem, anywhere],
        out_specs=(vmem, vmem),
        scratch_shapes=[pltpu.VMEM((8, KR, 2688), bf16), pltpu.VMEM((KR, 2688), f32), dma((8,))],
        compiler_params=pltpu.CompilerParams(vmem_limit_bytes=32 << 20),
        cost_estimate=pl.CostEstimate(flops=1 << 20, bytes_accessed=3 << 20, transcendentals=0),
    )(at_hbm(group_order), at_hbm(head_order), at_hbm(in_weight))
    gated, states, steps = pl.pallas_call(
        kernel,
        out_shape=(
            pltpu.VMEM((ROWS, HPG * HEAD), bf16),
            pltpu.VMEM((ROWS, 2 * N), bf16),
            pltpu.VMEM((HPG, ROWS), f32),
        ),
        in_specs=[anywhere, vmem, vmem, vmem, vmem, vmem],
        out_specs=(vmem, vmem, vmem),
        scratch_shapes=[
            pltpu.VMEM((5, D, CW), bf16),
            pltpu.VMEM((16, 8, KR, 128), bf16),
            pltpu.VMEM((8 * KR, 128), bf16),
            pltpu.VMEM((16 * KR, 128), bf16),
            pltpu.VMEM((HALO + ROWS, D), bf16),
            pltpu.VMEM((HALO + 2 * GRP, CW), f32),
            dma((7,)), dma((7,)), dma((6, 7)), dma((7,)), dma((8,)), dma((7, PIECES)), dma, dma, dma, dma,
        ],
        compiler_params=pltpu.CompilerParams(
            collective_id=0, has_side_effects=True, vmem_limit_bytes=56 << 20
        ),
        cost_estimate=pl.CostEstimate(
            flops=2 * ROWS * D * GW, bytes_accessed=6 << 20, transcendentals=ROWS * GW
        ),
    )(at_hbm(tokens), at_vmem(stage), at_vmem(stage_dt), conv_x, conv_bc, dt_bias.reshape(1, HPG))
    gated, states, steps = pl.pallas_call(
        finish,
        out_shape=(
            pltpu.HBM((ROWS, HPG * HEAD), bf16),
            pltpu.HBM((ROWS, 2 * N), bf16),
            pltpu.HBM((HPG, ROWS), f32),
        ),
        in_specs=[vmem, vmem, vmem],
        out_specs=(anywhere, anywhere, anywhere),
        scratch_shapes=[dma((7,))],
        cost_estimate=pl.CostEstimate(flops=0, bytes_accessed=3 << 20, transcendentals=0),
    )(at_vmem(gated), at_vmem(states), at_vmem(steps))
    return gated, states, steps.T


def solution(mesh):
    return jax.shard_map(
        on_device,
        mesh=mesh,
        in_specs=(
            P(("dp", "tensor"), None),
            P(("dp", "tensor"), None),
            P(),
            P(),
            P(None, "tensor"),
            P(None, "tensor"),
            P("tensor"),
        ),
        out_specs=(P("dp", "tensor"), P("dp", "tensor"), P("dp", "tensor")),
        check_vma=False,
    )
```

```python
import functools

import jax
import jax.numpy as jnp
from jax import lax
from jax.experimental import pallas as pl
from jax.experimental.pallas import tpu as pltpu
from jax.sharding import PartitionSpec as P

MESH = pl.DeviceIdType.MESH
HEAD = 64
HPG = 16
N = 256
GW = 2 * HPG * HEAD + 2 * N + HPG
D = 4096
ROWS = 1024
TOK = 128
PIECES = 4
PIECE = TOK // PIECES
HALF = {"b": slice(0, 256), "c": slice(256, 512)}
KB = 256
KR = 32
GRP = 256
HALO = 16
CW = 512
ORDER = ("dt", 0, 1, 2, 3, "b", "c")
BY_Z = ("b",)


def arrange(group_order, head_order, weight, stage, stage_dt, held, lined, sems):
    def fetch(slot):
        start = pl.multiple_of(20 * 128 * group_order[slot], 128)
        return pltpu.make_async_copy(weight.at[:, pl.ds(start, 2688)], held.at[slot], sems.at[slot])

    for slot in range(8):
        fetch(slot).start()

    lane = lax.broadcasted_iota(jnp.int32, (KR, 128), 1)
    ten = lax.axis_index("tensor")

    def line_up(slot):
        group = group_order[slot]
        fetch(slot).wait()
        for part in range(4):
            wide = held[slot, :, 640 * part : 640 * part + 768].astype(jnp.float32)
            lined[:, 640 * part : 640 * part + 640] = pltpu.roll(wide, (768 - 16 * group) % 768, 1)[:, :640]
        tile = pltpu.roll(held[slot, :, 2560:2688].astype(jnp.float32), (128 - 16 * group) % 128, 1)
        lined[:, 2560:2688] = jnp.where(lane < HPG, tile, 0.0)

    def head_tile(slot, base, first):
        parts = []
        for half in range(2):
            picked = head_order[slot, first + half]
            start = pl.multiple_of(base + 128 * (picked >> 1), 128)
            tile = lined[:, pl.ds(start, 128)]
            parts.append(jnp.where((picked & 1) == half, tile, pltpu.roll(tile, HEAD, 1)))
        return jnp.where(lane < HEAD, parts[0], parts[1]).astype(jnp.bfloat16)

    def make(chunk, slot, store):
        if chunk == "dt":
            source = jnp.full((128, 128), 128, jnp.int32)
            across = lax.broadcasted_iota(jnp.int32, (128, 128), 1)
            for j in range(HPG):
                source = jnp.where(across == j + HPG * ten, head_order[slot, j], source)
            down = lax.broadcasted_iota(jnp.int32, (128, 128), 0)
            pick = (down == source).astype(jnp.float32).astype(jnp.bfloat16)
            tile = lined[:, 2560:2688].astype(jnp.bfloat16)
            store(0, jnp.dot(tile, pick, preferred_element_type=jnp.float32).astype(jnp.bfloat16))
        elif chunk == 4:
            for tile in range(4):
                store(tile, lined[:, 2048 + 128 * tile : 2176 + 128 * tile].astype(jnp.bfloat16))
        else:
            for part in range(2):
                for pair in range(2):
                    store(2 * part + pair, head_tile(slot, 1024 * part, 4 * chunk + 2 * pair))

    def body(slot, carry):
        line_up(slot)

        def store_dt(tile, value):
            stage_dt[slot] = value

        make("dt", slot, store_dt)
        for chunk in range(5):

            def store(tile, value, chunk=chunk):
                stage[chunk, slot, :, 128 * tile : 128 * tile + 128] = value

            make(chunk, slot, store)
        return carry

    lax.fori_loop(0, 8, body, 0)


def kernel(
    tokens, stage, stage_dt, conv_x, conv_bc, dt_bias,
    gated, states, steps,
    panel, panel_dt, dt_in, dt_all, tok, proj,
    a2a_sem, z_sem, ring_sem, sib_sem, send_sem, t_sem, t_send, h_sem, h_send, own_sem,
):
    dp, ten = lax.axis_index("dp"), lax.axis_index("tensor")
    core, x, zh = dp % 2, (dp // 2) % 4, dp // 8
    y, zl = ten // 2, ten % 2

    def dp_of(zh_, x_, core_):
        return (zh_ * 4 + x_) * 2 + core_

    left, right, opposite = (x + 3) % 4, (x + 1) % 4, (x + 2) % 4
    up, down, far = (y + 1) % 4, (y + 3) % 4, (y + 2) % 4
    at_right = (dp_of(zh, right, core), ten)
    at_left = (dp_of(zh, left, core), ten)
    at_zh = (dp_of(1 - zh, x, core), ten)
    at_sib = (dp_of(zh, x, 1 - core), ten)
    at_up = (dp, up * 2 + zl)
    at_down = (dp, down * 2 + zl)
    at_zl = (dp, y * 2 + 1 - zl)
    after, before = ((dp + 1) % 16, ten), ((dp + 15) % 16, ten)

    load_t = pltpu.make_async_copy(tokens, tok.at[pl.ds(HALO + ten * TOK, TOK)], own_sem)
    load_t.start()

    barrier = pltpu.get_barrier_semaphore()
    for step in range(1, 8):
        pl.semaphore_signal(barrier, inc=1, device_id=(dp, (ten + step) % 8), device_id_type=MESH)
    for peer in (at_right, at_left, at_zh, at_sib, after, before):
        pl.semaphore_signal(barrier, inc=1, device_id=peer, device_id_type=MESH)

    def remote(src, dst, send, recv, peer):
        return pltpu.make_async_remote_copy(
            src_ref=src, dst_ref=dst, send_sem=send, recv_sem=recv, device_id=peer, device_id_type=MESH
        )

    def tok_rows(y_, zl_, piece):
        return tok.at[pl.ds(HALO + (y_ * 2 + zl_) * TOK + piece * PIECE, PIECE)]

    ZL, L0, R0, L1, R1, O0, O1 = range(7)
    arrives = {
        ZL: (y, 1 - zl), L0: (down, zl), R0: (up, zl), L1: (down, 1 - zl),
        R1: (up, 1 - zl), O0: (far, zl), O1: (far, 1 - zl),
    }
    waited = set()

    def tok_wait(*kinds, pieces=range(PIECES)):
        for kind in kinds:
            for piece in pieces:
                if (kind, piece) not in waited:
                    waited.add((kind, piece))
                    ref = tok_rows(*arrives[kind], piece)
                    pltpu.make_async_copy(ref, ref, t_sem.at[kind, piece]).wait()

    def tok_send(ref, dst, kind, piece, peer):
        remote(ref, dst, t_send, t_sem.at[kind, piece], peer).start()

    def slot(q):
        piece = PIECES - 1 - q % PIECES
        if q < PIECES:
            src, dst = tokens.at[pl.ds(piece * PIECE, PIECE)], tok_rows(y, zl, piece)
            tok_send(src, dst, L0, piece, at_up)
            tok_send(src, dst, R0, piece, at_down)
        elif q < 2 * PIECES:
            tok_wait(ZL, pieces=(piece,))
            ref = tok_rows(y, 1 - zl, piece)
            tok_send(ref, ref, L1, piece, at_up)
            tok_send(ref, ref, R1, piece, at_down)
        else:
            tok_wait(L0, R1, pieces=(piece,))
            ref = tok_rows(down, zl, piece)
            tok_send(ref, ref, O0, piece, at_up)
            ref = tok_rows(up, 1 - zl, piece)
            tok_send(ref, ref, O1, piece, at_down)

    def across(piece):
        src, dst = tokens.at[pl.ds(piece * PIECE, PIECE)], tok_rows(y, zl, piece)
        tok_send(src, dst, ZL, piece, at_zl)

    def tok_near():
        tok_wait(ZL, L0, R0, L1, R1)

    def tok_far():
        tok_wait(O0, O1)

    head = tok.at[pl.ds(0, HALO)]

    def halo_send(where, src, *peers):
        @pl.when(where)
        def _():
            for peer in peers:
                remote(src, head, h_send, h_sem, peer).start()

    def halo_wait(where):
        @pl.when(jnp.logical_and(where, dp > 0))
        def _():
            pltpu.make_async_copy(head, head, h_sem).wait()

    def halo_sent(where, count):
        @pl.when(where)
        def _():
            for _ in range(count):
                pltpu.make_async_copy(head, head, h_send).wait()

    halo_first = jnp.logical_and(ten == 7, dp < 15)
    halo_a = ten == 7
    halo_b = ten == 6
    halo_c = ten == 1
    halo_d = ten == 4
    halo_e = ten == 0
    halo_rest = jnp.logical_or(ten == 5, y == 1)
    inner = dp > 0

    @pl.when(dp == 0)
    def _():
        tok[0:HALO, :] = jnp.zeros((HALO, D), jnp.bfloat16)

    def rows_of(chunk, start, size):
        if chunk == "dt":
            return dt_all.at[pl.ds(start, size)]
        if chunk in ("b", "c"):
            return panel.at[4, pl.ds(start, size), HALF[chunk]]
        return panel.at[chunk, pl.ds(start, size)]

    def sem_of(chunk):
        return ORDER.index(chunk)

    def height(chunk):
        return KR if chunk == "dt" else KB

    def block(chunk, zh_, x_, core_):
        return rows_of(chunk, dp_of(zh_, x_, core_) * height(chunk), height(chunk))

    def prepare(chunk):
        if chunk == "dt":
            dst, sent = dt_in.at[pl.ds(ten * KR, KR)], send_sem.at[len(ORDER)]
        else:
            dst, sent = rows_of(chunk, dp * KB + ten * KR, KR), send_sem.at[sem_of(chunk)]
        sem = a2a_sem.at[sem_of(chunk)]

        def source(slot):
            if chunk == "dt":
                return stage_dt.at[slot]
            if chunk in ("b", "c"):
                return stage.at[4, slot, :, HALF[chunk]]
            return stage.at[chunk, slot]

        for step in range(1, 8):
            slot = (ten + step) % 8
            remote(source(slot), dst, sent, sem, (dp, slot)).start()
        pltpu.make_async_copy(source(ten), dst, sem).start()

    def send(chunk, ref, recv, peer):
        remote(ref, ref, send_sem.at[sem_of(chunk)], recv.at[sem_of(chunk)], peer).start()

    def wait(chunk, ref, sem):
        pltpu.make_async_copy(ref, ref, sem.at[sem_of(chunk)]).wait()

    def ring(kind):
        return ring_sem.at[kind]

    RL0, RR0, RL1, RR1, RO0, RO1 = range(6)

    def s_z(chunk):
        send(chunk, block(chunk, zh, x, core), z_sem, at_zh)

    def s_ready(chunk):
        if chunk == "dt":
            pltpu.make_async_copy(dt_in, dt_in, a2a_sem.at[sem_of(chunk)]).wait()
            total = dt_in[0:KR, :].astype(jnp.float32)
            for sender in range(1, 8):
                total = total + dt_in[KR * sender : KR * sender + KR, :].astype(jnp.float32)
            dt_all[pl.ds(dp * KR, KR), :] = total.astype(jnp.bfloat16)
        else:
            wait(chunk, block(chunk, zh, x, core), a2a_sem)

    def s_own(chunk):
        ref = block(chunk, zh, x, core)
        send(chunk, ref, ring(RL0), at_right)
        send(chunk, ref, ring(RR0), at_left)
        send(chunk, ref, sib_sem, at_sib)

    def s_pair(chunk):
        ref = block(chunk, 1 - zh, x, core)
        wait(chunk, ref, z_sem)
        if chunk not in BY_Z:
            send(chunk, ref, ring(RL1), at_right)
            send(chunk, ref, ring(RR1), at_left)
        send(chunk, ref, sib_sem, at_sib)

    def s_right(chunk):
        ref = block(chunk, zh, right, core)
        wait(chunk, ref, ring(RR0))
        if chunk in BY_Z:
            send(chunk, ref, ring(RR1), at_zh)
        send(chunk, ref, sib_sem, at_sib)

    def s_near(chunk):
        ref = block(chunk, zh, left, core)
        wait(chunk, ref, ring(RL0))
        send(chunk, ref, ring(RO0), at_right)
        if chunk in BY_Z:
            send(chunk, ref, ring(RL1), at_zh)
        send(chunk, ref, sib_sem, at_sib)
        if chunk in BY_Z:
            s_right(chunk)

    def s_next(chunk):
        ref = block(chunk, 1 - zh, right, core)
        wait(chunk, ref, ring(RR1))
        send(chunk, ref, ring(RO1), at_left)
        send(chunk, ref, sib_sem, at_sib)

    def s_far(chunk):
        if chunk not in BY_Z:
            s_right(chunk)
        ref = block(chunk, 1 - zh, left, core)
        wait(chunk, ref, ring(RL1))
        send(chunk, ref, sib_sem, at_sib)
        ref = block(chunk, zh, opposite, core)
        wait(chunk, ref, ring(RO0))
        send(chunk, ref, sib_sem, at_sib)
        ref = block(chunk, 1 - zh, opposite, core)
        wait(chunk, ref, ring(RO1))
        send(chunk, ref, sib_sem, at_sib)

    def s_sib(chunk):
        wait(chunk, rows_of(chunk, 0, 8 * height(chunk)), sib_sem)

    def unpack():
        packed = dt_all[...].astype(jnp.float32)
        for sender in range(8):
            turned = pltpu.roll(packed, (128 - HPG * sender) % 128, 1)
            panel_dt[:, sender] = turned.reshape(16, KR, 128).astype(jnp.bfloat16)

    def silu(v):
        return 0.5 * v * (1.0 + jnp.tanh(0.5 * v))

    def rounded(v):
        return v.astype(jnp.bfloat16).astype(jnp.float32)

    def conv(taps, size, col):
        total = taps[0:1, :] * proj[pl.ds(HALO - 3, size), col : col + 256]
        for k in range(1, 4):
            total = total + taps[k : k + 1, :] * proj[pl.ds(HALO - 3 + k, size), col : col + 256]
        return total

    def unit(start, size, chunk):
        lhs = tok[pl.ds(start, HALO + size), :]
        into = pl.ds(0, HALO + size)
        if chunk in ("b", "c"):
            cols = HALF[chunk]
            spot = HALF["b" if (start // size) % 2 else "c"]
            proj[into, spot] = rounded(jnp.dot(lhs, panel[4, :, cols], preferred_element_type=jnp.float32))
            states[pl.ds(start, size), cols] = silu(conv(conv_bc[:, cols], size, spot.start)).astype(jnp.bfloat16)
        else:
            for half in HALF.values():
                proj[into, half] = rounded(jnp.dot(lhs, panel[chunk, :, half], preferred_element_type=jnp.float32))
            cols = slice(256 * chunk, 256 * chunk + 256)
            value = silu(conv(conv_x[:, cols], size, 256)) * silu(proj[pl.ds(HALO, size), 0:256])
            gated[pl.ds(start, size), cols] = value.astype(jnp.bfloat16)

    def whole(chunk, steps=range(4)):
        for step in steps:
            unit(step * GRP, GRP, chunk)

    def unit_dt(group):
        start = pl.multiple_of(group * GRP, GRP)
        raw = rounded(jnp.dot(tok[pl.ds(start + HALO, GRP), :], panel_dt[...].reshape(D, 128), preferred_element_type=jnp.float32))
        value = (raw[:, :HPG] + dt_bias[...]).T
        steps[:, pl.ds(start, GRP)] = jnp.maximum(value, 0.0) + jnp.log1p(jnp.exp(-jnp.abs(value)))

    def units(places, *chunks):
        for place in places:
            for chunk in chunks:
                if chunk == "dt":
                    unit_dt(groups[place])
                else:
                    unit(pl.multiple_of(groups[place] * GRP, GRP), GRP, chunk)

    groups = (y, up, down, far)

    pl.semaphore_wait(barrier, 13)
    prepare(0)
    halo_send(halo_first, tokens.at[pl.ds(TOK - HALO, HALO)], after)
    prepare(1)
    prepare("dt")
    s_ready(0)
    s_z(0)
    s_own(0)
    prepare(2)
    slot(0)
    s_ready(1)
    s_own(1)
    s_near(0)
    across(3)
    slot(1)
    halo_wait(halo_a)
    halo_send(jnp.logical_and(halo_a, inner), head, at_zl, at_up, at_down)
    s_pair(0)
    s_z(1)
    s_ready("dt")
    s_z("dt")
    s_own("dt")
    prepare(3)
    slot(2)
    across(2)
    s_next(0)
    s_near(1)
    across(1)
    s_pair(1)
    s_ready(2)
    s_own(2)
    s_z(2)
    slot(3)
    halo_wait(halo_b)
    halo_send(jnp.logical_and(halo_b, inner), head, at_up, at_down)
    slot(4)
    prepare("b")
    s_near("dt")
    s_pair("dt")
    across(0)
    slot(5)
    s_next(1)
    s_near(2)
    slot(6)
    prepare("c")
    s_pair(2)
    s_ready(3)
    s_own(3)
    s_z(3)
    slot(7)
    s_next("dt")
    s_far(0)
    halo_wait(jnp.logical_or(halo_c, halo_d))
    halo_send(jnp.logical_and(halo_c, inner), head, at_up)
    halo_send(jnp.logical_and(halo_d, inner), head, at_down)
    slot(8)
    s_next(2)
    s_ready("b")
    s_own("b")
    load_t.wait()
    halo_wait(halo_e)
    tok_wait(ZL)
    tok_wait(L0, L1, pieces=(3,))
    s_sib(0)
    units((0,), 0)
    s_near(3)
    s_z("b")
    s_far(1)
    s_pair(3)
    slot(9)
    tok_wait(L0, R0, L1, R1)
    units((1,), 0)
    s_ready("c")
    s_own("c")
    s_z("c")
    s_far("dt")
    slot(10)
    s_sib(1)
    units((0, 1), 1)
    s_near("b")
    s_far(2)
    slot(11)
    tok_wait(O0, O1, pieces=(3,))
    halo_wait(halo_rest)
    units((2,), 0, 1)
    s_next(3)
    s_sib("dt")
    unpack()
    units((0, 1, 2), "dt")
    s_sib(2)
    units((0, 1, 2), 2)
    s_near("c")
    s_pair("b")
    s_pair("c")
    s_far(3)
    s_next("b")
    tok_far()
    units((3,), "dt", 0, 1)
    s_next("c")
    s_sib(3)
    units((3,), 2)
    whole(3, (0, 1))
    s_far("b")
    s_far("c")
    whole(3, (2, 3))
    s_sib("b")
    whole("b")
    s_sib("c")
    whole("c")

    pltpu.make_async_copy(tok.at[pl.ds(0, 7 * TOK)], tok.at[pl.ds(0, 7 * TOK)], t_send).wait()

    halo_sent(halo_first, 1)
    halo_sent(jnp.logical_and(halo_a, inner), 3)
    halo_sent(jnp.logical_and(halo_b, inner), 2)
    halo_sent(jnp.logical_and(jnp.logical_or(halo_c, halo_d), inner), 1)

    for chunk in ORDER[1:]:
        wait(chunk, rows_of(chunk, 0, 15 * KB + 7 * KR), send_sem)
    wait("dt", rows_of("dt", 0, 15 * KR), send_sem)
    ref = dt_in.at[pl.ds(0, 7 * KR)]
    pltpu.make_async_copy(ref, ref, send_sem.at[len(ORDER)]).wait()


def finish(gated_v, states_v, steps_v, gated, states, steps, sems):
    copies = [pltpu.make_async_copy(steps_v, steps, sems.at[6])]
    for part in range(4):
        rows = pl.ds(GRP * part, GRP)
        copies.append(pltpu.make_async_copy(gated_v.at[rows], gated.at[rows], sems.at[part]))
    for part in range(2):
        rows = pl.ds(2 * GRP * part, 2 * GRP)
        copies.append(pltpu.make_async_copy(states_v.at[rows], states.at[rows], sems.at[4 + part]))
    for copy in copies:
        copy.start()
    for copy in copies:
        copy.wait()


def on_device(tokens, in_weight, group_order, head_order, conv_x, conv_bc, dt_bias):
    vmem, smem, anywhere = (
        pl.BlockSpec(memory_space=pltpu.VMEM),
        pl.BlockSpec(memory_space=pltpu.SMEM),
        pl.BlockSpec(memory_space=pl.ANY),
    )
    dma = pltpu.SemaphoreType.DMA
    bf16, f32 = jnp.bfloat16, jnp.float32
    def at_vmem(value):
        return pltpu.with_memory_space_constraint(value, pltpu.VMEM)

    def at_hbm(value):
        return pltpu.with_memory_space_constraint(value, pltpu.HBM)

    stage, stage_dt = pl.pallas_call(
        arrange,
        out_shape=(pltpu.VMEM((5, 8, KR, CW), bf16), pltpu.VMEM((8, KR, 128), bf16)),
        in_specs=[smem, smem, anywhere],
        out_specs=(vmem, vmem),
        scratch_shapes=[pltpu.VMEM((8, KR, 2688), bf16), pltpu.VMEM((KR, 2688), f32), dma((8,))],
        compiler_params=pltpu.CompilerParams(vmem_limit_bytes=32 << 20),
        cost_estimate=pl.CostEstimate(flops=1 << 20, bytes_accessed=3 << 20, transcendentals=0),
    )(at_hbm(group_order), at_hbm(head_order), at_hbm(in_weight))
    gated, states, steps = pl.pallas_call(
        kernel,
        out_shape=(
            pltpu.VMEM((ROWS, HPG * HEAD), bf16),
            pltpu.VMEM((ROWS, 2 * N), bf16),
            pltpu.VMEM((HPG, ROWS), f32),
        ),
        in_specs=[anywhere, vmem, vmem, vmem, vmem, vmem],
        out_specs=(vmem, vmem, vmem),
        scratch_shapes=[
            pltpu.VMEM((5, D, CW), bf16),
            pltpu.VMEM((16, 8, KR, 128), bf16),
            pltpu.VMEM((8 * KR, 128), bf16),
            pltpu.VMEM((16 * KR, 128), bf16),
            pltpu.VMEM((HALO + ROWS, D), bf16),
            pltpu.VMEM((HALO + 2 * GRP, CW), f32),
            dma((7,)), dma((7,)), dma((6, 7)), dma((7,)), dma((8,)), dma((7, PIECES)), dma, dma, dma, dma,
        ],
        compiler_params=pltpu.CompilerParams(
            collective_id=0, has_side_effects=True, vmem_limit_bytes=56 << 20
        ),
        cost_estimate=pl.CostEstimate(
            flops=2 * ROWS * D * GW, bytes_accessed=6 << 20, transcendentals=ROWS * GW
        ),
    )(at_hbm(tokens), at_vmem(stage), at_vmem(stage_dt), conv_x, conv_bc, dt_bias.reshape(1, HPG))
    gated, states, steps = pl.pallas_call(
        finish,
        out_shape=(
            pltpu.HBM((ROWS, HPG * HEAD), bf16),
            pltpu.HBM((ROWS, 2 * N), bf16),
            pltpu.HBM((HPG, ROWS), f32),
        ),
        in_specs=[vmem, vmem, vmem],
        out_specs=(anywhere, anywhere, anywhere),
        scratch_shapes=[dma((7,))],
        cost_estimate=pl.CostEstimate(flops=0, bytes_accessed=3 << 20, transcendentals=0),
    )(at_vmem(gated), at_vmem(states), at_vmem(steps))
    return gated, states, steps.T


def solution(mesh):
    return jax.shard_map(
        on_device,
        mesh=mesh,
        in_specs=(
            P(("dp", "tensor"), None),
            P(("dp", "tensor"), None),
            P(),
            P(),
            P(None, "tensor"),
            P(None, "tensor"),
            P("tensor"),
        ),
        out_specs=(P("dp", "tensor"), P("dp", "tensor"), P("dp", "tensor")),
        check_vma=False,
    )
```
